128 devices in a mesh: fsdp: 8 (over y, core), expert: 16 (over z, x).
Axes of the slice: x: 4, y: 4, z: 4, core: 2. Of those that a mesh axis runs over, the one named last changes fastest.
Arguments:
- hidden_in: bfloat16 [16, 1280, 1024], P('expert', 'fsdp'), may hold values from -6 to 6
- grad_out: bfloat16 [16, 1280, 1024], P('expert', 'fsdp'), may hold values from -6 to 6
- lengths: int32 [16, 3], P('expert'), may hold values from 1 to 1278, as said below
- experts: int32 [16, 1280, 8], P('expert', 'fsdp'), may hold values from 0 to 31, all different within a row; in each aligned block of 160 rows (0 to 159, 160 to 319, ..., all dimensions but the last counted through in order) at most 50 rows name the same one
- gain_attn: bfloat16 [1024], P('fsdp'), may hold values from 0.5 to 1.5
- w_query: bfloat16 [1024, 1024], P('fsdp'), may hold values from -0.1875 to 0.1875
- key_weight: bfloat16 [1024, 512], P('fsdp'), may hold values from -0.1875 to 0.1875
- value_weight: bfloat16 [1024, 512], P('fsdp'), may hold values from -0.1875 to 0.1875
- w_out: bfloat16 [1024, 1024], P('fsdp'), may hold values from -0.75 to 0.75
- gain_moe: bfloat16 [1024], P('fsdp'), may hold values from 0.5 to 1.5
- w_router: bfloat16 [1024, 32], P('fsdp'), may hold values from -0.09375 to 0.09375
- expert_gate: bfloat16 [32, 1024, 512], P('expert', 'fsdp'), may hold values from -0.1875 to 0.1875
- expert_up: bfloat16 [32, 1024, 512], P('expert', 'fsdp'), may hold values from -0.1875 to 0.1875
- expert_down: bfloat16 [32, 512, 1024], P('expert', 'fsdp'), may hold values from -1 to 1
Outputs:
- hidden_out: bfloat16 [16, 1280, 1024], P('expert', 'fsdp')
- grad_hidden_in: bfloat16 [16, 1280, 1024], P('expert', 'fsdp')
- grad_gain_attn: float32 [1024], P('fsdp')
- grad_w_query: float32 [1024, 1024], P('fsdp')
- grad_w_key: float32 [1024, 512], P('fsdp')
- grad_w_value: float32 [1024, 512], P('fsdp')
- grad_w_out: float32 [1024, 1024], P('fsdp')
- grad_gain_moe: float32 [1024], P('fsdp')
- grad_w_router: float32 [1024, 32], P('fsdp')
- grad_expert_gate: float32 [32, 1024, 512], P('expert', 'fsdp')
- grad_expert_up: float32 [32, 1024, 512], P('expert', 'fsdp')
- grad_expert_down: float32 [32, 512, 1024], P('expert', 'fsdp')
The draws below stay inside these ranges and needn't reach their ends.
Inputs may be any that keep to these rules, and one draw needn't show every extreme that they name: In each pack the 3 lengths add up to 1280; one of them, at a place drawn from the seed, begins within the first 160 tokens and ends within the last 160; in the first pack every other length is 1. Each token names 8 different experts; among the rows of one device no expert is named more than 50 times, a bound that some block reaches.
All inputs are finite; a program needn't handle non-finite values.
Results may differ from the reference program's by a relative error of at most 0.028.
Values may be sent and summed in bfloat16 or wider, within the bound.
A program may use at most 192 MiB of HBM per device.

```python
import math
import jax
import jax.numpy as jnp
import numpy as np
from jax import lax

MODEL_SIZE = 1024
QUERY_HEADS = 16
KEY_VALUE_HEADS = 8
HEAD_SIZE = 64
FF = 512
TOPK = 8
NSEQ = 3
PACK_TOKENS = 1280
ROWS = 160
PACKS = 16
EXPERTS = 32
CAP = 50
N_FSDP = 8


def draw_lengths(key, part):
    key = jax.random.fold_in(key, 11)
    first_key, second_key = jax.random.split(key)
    short_len = jax.random.randint(first_key, (PACKS, NSEQ), 1, max(1, ROWS // 4) + 1)
    first_pack = jnp.arange(PACKS)[:, None] == 0
    short_len = jnp.where(first_pack, 1, short_len)
    long_place = jax.random.randint(second_key, (PACKS, 1), 0, NSEQ)
    column = jnp.arange(NSEQ)[None, :]
    is_long = column == long_place
    others = jnp.sum(jnp.where(is_long, 0, short_len), axis=1, keepdims=True)
    return jnp.where(is_long, PACK_TOKENS - others, short_len).astype(jnp.int32)


def steps_of(own_key, shape, shards, smallest, top_value):
    loudness, own = 1.0, jax.random.fold_in(own_key, 6)
    for axis_at, shards_of in shards:
        draws = jnp.exp(jax.random.uniform(jax.random.fold_in(own, axis_at), (shards_of,), jnp.float32, smallest / len(shards), top_value / len(shards)))
        loudness = loudness * jnp.repeat(draws, shape[axis_at] // shards_of).reshape([-1 if axis == axis_at else 1 for axis in range(len(shape))])
    return loudness


def shared_out(rng, own, number, rows, number_of, top, bound, lean):
    sequence = jax.random.permutation(rng, number_of)
    crowded, ordinary = portions_of(number_of, rows * top, bound, lean, True), portions_of(number_of, rows * top, bound, lean, False)
    places = jnp.arange(number_of)

    def named(sizes, offset_by):
        used = int((sizes > 0).sum())
        fixed = max(1, used // 4)
        shifted = fixed + (places - fixed + offset_by * (used - fixed)) % max(1, number_of - fixed)
        return jnp.zeros((number_of,), jnp.int32).at[sequence[jnp.where(places < fixed, places, shifted)]].set(jnp.asarray(sizes, jnp.int32))

    sizes = jnp.where(number % 4 == 0, named(crowded, number // 4), named(ordinary, number - number // 4 - 1))
    mixed = jax.random.permutation(jax.random.fold_in(own, 3), number_of)
    giver, receiver = mixed[0:number_of // 2 * 2:2], mixed[1:number_of // 2 * 2:2]
    margin = jnp.minimum(sizes[giver] - 1, bound - sizes[receiver]) // 2
    margin = jnp.where((giver == sequence[0]) | (receiver == sequence[0]) | (sizes[receiver] == 0), 0, jnp.maximum(margin, 0))
    shifted = jax.random.randint(jax.random.fold_in(own, 4), (number_of // 2,), 0, 1 << 20) % (margin + 1)
    sizes = sizes.at[giver].add(-shifted).at[receiver].add(shifted)
    members = jnp.searchsorted(jnp.cumsum(sizes), jnp.arange(rows * top), side="right").astype(jnp.int32)
    grid = members.reshape(top, rows).T
    grid = grid[jax.random.permutation(jax.random.fold_in(own, 1), rows)]
    offset_by = jax.random.randint(jax.random.fold_in(own, 2), (rows, 1), 0, top)
    return jnp.take_along_axis(grid, (jnp.arange(top)[None, :] + offset_by) % top, axis=1)


def portions_of(amount, total, limit, slope, full):
    loads = [(1 << 20) // math.isqrt(grade ** slope) + 1 for grade in range(1, amount + 1)]
    largest = limit if full else min(limit, max(-(-total // amount), total * loads[0] // sum(loads)))
    least = 1 if total - largest >= amount - 1 else 0
    given, rest = [largest] + [least] * (amount - 1), total - largest - least * (amount - 1)
    while rest > 0:
        free = [i for i in range(1, amount) if given[i] < largest] or [i for i in range(1, amount) if given[i] < limit]
        pool, budget = sum([loads[i] for i in free]), rest
        for i in free:
            extra = min(limit - given[i], max(1, budget * loads[i] // pool), rest)
            given[i] = given[i] + extra
            rest = rest - extra
    return np.array(given)


def bell_draw(key, dims, spread, limit, cuts=(), kind=jnp.bfloat16):
    values = spread * jax.random.normal(key, dims, jnp.float32)
    if cuts:
        values = values * steps_of(key, dims, cuts, -0.22, 0.18)
    return jnp.clip(values, -limit, limit).astype(kind)


def setup_inputs(seed: int = 0) -> dict:
    key_of = jax.random.split(jax.random.key(seed), 15)
    hidden_in = bell_draw(key_of[0], (PACKS, PACK_TOKENS, MODEL_SIZE), 1.0, 6.0, ((0, 16), (1, 8)))
    grad_out = bell_draw(key_of[1], (PACKS, PACK_TOKENS, MODEL_SIZE), 1.0, 6.0, ((0, 16), (1, 8)))
    lengths = draw_lengths(jax.random.fold_in(key_of[14], 71), 0)
    experts_keys = jax.random.split(jax.random.fold_in(key_of[3], 1), PACKS * PACK_TOKENS // ROWS)
    experts_turns = jax.random.permutation(jax.random.fold_in(key_of[3], 3), PACKS * PACK_TOKENS // ROWS)
    experts = jax.vmap(lambda own, number: shared_out(jax.random.fold_in(key_of[3], 2), own, number, ROWS, EXPERTS, TOPK, CAP, 2))(experts_keys, experts_turns).reshape((PACKS, PACK_TOKENS, TOPK))
    gain_attn = jnp.clip(1.0 + 0.1 * jax.random.normal(key_of[4], (MODEL_SIZE,), jnp.float32), 0.5, 1.5).astype(jnp.bfloat16)
    w_query = bell_draw(key_of[5], (MODEL_SIZE, QUERY_HEADS * HEAD_SIZE), MODEL_SIZE ** -0.5, 0.1875, ((0, 8),))
    key_weight = bell_draw(key_of[6], (MODEL_SIZE, KEY_VALUE_HEADS * HEAD_SIZE), MODEL_SIZE ** -0.5, 0.1875, ((0, 8),))
    value_weight = bell_draw(key_of[7], (MODEL_SIZE, KEY_VALUE_HEADS * HEAD_SIZE), MODEL_SIZE ** -0.5, 0.1875, ((0, 8),))
    w_out = bell_draw(key_of[8], (QUERY_HEADS * HEAD_SIZE, MODEL_SIZE), (QUERY_HEADS * HEAD_SIZE // 16) ** -0.5, 0.75, ((0, 8),))
    gain_moe = jnp.clip(1.0 + 0.1 * jax.random.normal(key_of[9], (MODEL_SIZE,), jnp.float32), 0.5, 1.5).astype(jnp.bfloat16)
    w_router = bell_draw(key_of[10], (MODEL_SIZE, EXPERTS), (4 * MODEL_SIZE) ** -0.5, 0.09375, ((0, 8),))
    expert_gate = bell_draw(key_of[11], (EXPERTS, MODEL_SIZE, FF), MODEL_SIZE ** -0.5, 0.1875, ((0, 16), (1, 8)))
    expert_up = bell_draw(key_of[12], (EXPERTS, MODEL_SIZE, FF), MODEL_SIZE ** -0.5, 0.1875, ((0, 16), (1, 8)))
    expert_down = bell_draw(key_of[13], (EXPERTS, FF, MODEL_SIZE), (FF // 16) ** -0.5, 1.0, ((0, 16), (1, 8)))
    return {"hidden_in": hidden_in, "grad_out": grad_out, "lengths": lengths, "experts": experts, "gain_attn": gain_attn, "w_query": w_query, "key_weight": key_weight, "value_weight": value_weight, "w_out": w_out, "gain_moe": gain_moe, "w_router": w_router, "expert_gate": expert_gate, "expert_up": expert_up, "expert_down": expert_down}


EPS = 1e-06
BASE = 10000.0

@jax.custom_vjp
def reduced_precision(v):
    return lax.optimization_barrier(v.astype(jnp.bfloat16)).astype(jnp.float32)

@jax.custom_vjp
def reduced_backward(v):
    return v

def low_keep(v):
    return (reduced_precision(v), None)

def low_pass(kept, grad):
    return (grad,)

def back_keep(v):
    return (v, None)

def back_low(kept, grad):
    return (reduced_precision(grad),)
reduced_precision.defvjp(low_keep, low_pass)
reduced_backward.defvjp(back_keep, back_low)

def matrix_product(left_op, right_op):
    return jnp.dot(left_op, right_op, precision=lax.Precision.HIGHEST, preferred_element_type=jnp.float32)

def batched(pattern, left_op, right_op):
    return jnp.einsum(pattern, left_op, right_op, precision=lax.Precision.HIGHEST, preferred_element_type=jnp.float32)

def rms_norm(inputs, gain_vec):
    inverse_rms = lax.rsqrt(lax.optimization_barrier(jnp.mean(inputs * inputs, axis=-1, keepdims=True)) + EPS)
    return inputs * inverse_rms * gain_vec

def places(seq_lengths):
    seq_ends = jnp.cumsum(seq_lengths, dtype=jnp.int32)
    starts = seq_ends - seq_lengths
    token_index = jnp.arange(PACK_TOKENS, dtype=jnp.int32)[:, None]
    inside = ((token_index >= starts[None, :]) & (token_index < seq_ends[None, :])).astype(jnp.int32)
    segment = lax.optimization_barrier(jnp.sum(inside * jnp.arange(NSEQ, dtype=jnp.int32)[None, :], axis=1)).astype(jnp.int32)
    offset = lax.optimization_barrier(jnp.sum(inside * (token_index - starts[None, :]), axis=1)).astype(jnp.int32)
    return (segment, offset)

def rotary(offset):
    half_dim = HEAD_SIZE // 2
    frequency = BASE ** (-2.0 * jnp.arange(half_dim, dtype=jnp.float32) / HEAD_SIZE)
    angles = offset.astype(jnp.float32)[:, None] * frequency[None, :]
    angles = jnp.concatenate([angles, angles], axis=1)
    return (jnp.cos(angles), jnp.sin(angles))

def apply_rotation(vector, cosine_table, sine_lookup):
    half_dim = HEAD_SIZE // 2
    swapped = jnp.concatenate([-vector[..., half_dim:], vector[..., :half_dim]], axis=-1)
    return vector * cosine_table[:, None, :] + swapped * sine_lookup[:, None, :]

def destinations(picked_ids):
    flat_ids = picked_ids.reshape(N_FSDP, ROWS * TOPK)
    onehot = (flat_ids[:, :, None] == jnp.arange(EXPERTS, dtype=jnp.int32)[None, None, :]).astype(jnp.int32)
    counted = jnp.cumsum(onehot, axis=1, dtype=jnp.int32)
    slot_index = (lax.optimization_barrier(jnp.sum(counted * onehot, axis=2)) - 1).astype(jnp.int32)
    shard_index = jnp.arange(N_FSDP, dtype=jnp.int32)[:, None]
    return (flat_ids * (N_FSDP * CAP) + shard_index * CAP + slot_index).reshape(PACK_TOKENS * TOPK)

def layer_pack(inputs, seq_lengths, picked_ids, weight_set):
    gain_attn, w_query, key_weight, value_weight, w_out, gain_moe, w_router, expert_gate, expert_up, expert_down = weight_set
    segment, offset = places(seq_lengths)
    cosine_table, sine_lookup = rotary(offset)
    rescaled_hidden = reduced_precision(rms_norm(inputs, gain_attn))
    query_rows = reduced_backward(matrix_product(rescaled_hidden, w_query)).reshape(PACK_TOKENS, QUERY_HEADS, HEAD_SIZE)
    key_row_block = reduced_backward(matrix_product(rescaled_hidden, key_weight)).reshape(PACK_TOKENS, KEY_VALUE_HEADS, HEAD_SIZE)
    value_rows = reduced_precision(reduced_backward(matrix_product(rescaled_hidden, value_weight))).reshape(PACK_TOKENS, KEY_VALUE_HEADS, HEAD_SIZE)
    query_rows = reduced_precision(apply_rotation(query_rows, cosine_table, sine_lookup)).reshape(PACK_TOKENS, KEY_VALUE_HEADS, QUERY_HEADS // KEY_VALUE_HEADS, HEAD_SIZE)
    key_row_block = reduced_precision(apply_rotation(key_row_block, cosine_table, sine_lookup))
    scores = reduced_backward(batched('qhgd,khd->hgqk', query_rows, key_row_block)) * HEAD_SIZE ** (-0.5)
    position = jnp.arange(PACK_TOKENS, dtype=jnp.int32)
    allowed = (segment[:, None] == segment[None, :]) & (position[None, :] <= position[:, None])
    scores = jnp.where(allowed, scores, -1e+30)
    weights_soft = reduced_precision(jax.nn.softmax(scores, axis=-1))
    attended = batched('hgqk,khd->qhgd', weights_soft, value_rows).reshape(PACK_TOKENS, QUERY_HEADS * HEAD_SIZE)
    attended = reduced_precision(reduced_backward(attended))
    hidden = inputs + reduced_backward(matrix_product(attended, w_out))
    routed = reduced_precision(rms_norm(hidden, gain_moe))
    logits = reduced_backward(matrix_product(routed, w_router))
    chosen = jnp.take_along_axis(logits, picked_ids, axis=1)
    gate_probs = jax.nn.softmax(chosen, axis=-1)
    targets = destinations(picked_ids)
    source_rows = jnp.full((EXPERTS * N_FSDP * CAP,), PACK_TOKENS, jnp.int32)
    source_rows = source_rows.at[targets].set(jnp.arange(PACK_TOKENS * TOPK, dtype=jnp.int32) // TOPK)
    padded = jnp.concatenate([routed, jnp.zeros((1, MODEL_SIZE), jnp.float32)], axis=0)
    rows_in = reduced_backward(padded[source_rows]).reshape(EXPERTS, N_FSDP * CAP, MODEL_SIZE)
    gate_part = reduced_backward(batched('erd,edf->erf', rows_in, expert_gate))
    up_part = reduced_backward(batched('erd,edf->erf', rows_in, expert_up))
    inner_act = reduced_precision(jax.nn.silu(gate_part) * up_part)
    result = reduced_precision(reduced_backward(batched('erf,efd->erd', inner_act, expert_down)))
    returned = result.reshape(EXPERTS * N_FSDP * CAP, MODEL_SIZE)[targets].reshape(PACK_TOKENS, TOPK, MODEL_SIZE)
    return hidden + lax.optimization_barrier(jnp.sum(gate_probs[:, :, None] * returned, axis=1))

def reference(hidden_in, grad_out, lengths, experts, gain_attn, w_query, key_weight, value_weight, w_out, gain_moe, w_router, expert_gate, expert_up, expert_down):
    float_weights = tuple((weight.astype(jnp.float32) for weight in (gain_attn, w_query, key_weight, value_weight, w_out, gain_moe, w_router, expert_gate, expert_up, expert_down)))

    def whole_layer(inputs, weight_set):

        def one_pack(items):
            return layer_pack(items[0], items[1], items[2], weight_set)
        return lax.map(jax.checkpoint(one_pack), (inputs, lengths, experts))
    output, pullback = jax.vjp(whole_layer, hidden_in.astype(jnp.float32), float_weights)
    grad_in, grad_weights = pullback(grad_out.astype(jnp.float32))
    return (output.astype(jnp.bfloat16), grad_in.astype(jnp.bfloat16), grad_weights[0], grad_weights[1], grad_weights[2], grad_weights[3], grad_weights[4], grad_weights[5], grad_weights[6], grad_weights[7], grad_weights[8], grad_weights[9])
```

```python
import functools

import jax
import jax.numpy as jnp
from jax import lax
from jax.experimental import pallas as pl
from jax.experimental.pallas import tpu as pltpu
from jax.sharding import PartitionSpec as P

MESH = pl.DeviceIdType.MESH
QUERY_HEADS = 16
KEY_VALUE_HEADS = 8
HEAD_SIZE = 64
TOPK = 8
EXPERTS = 32
ROWS = 160
SLOTS = 64
LANES = 256
WIDTH = 1024
EPS = 1e-06
BASE = 10000.0
BF = jnp.bfloat16
F32 = jnp.float32


class Event:
    def __init__(self, copy, arriving):
        self.copy, self.arriving = copy, arriving

    def arrived(self):
        self.arriving.wait_recv()


class Net:
    def __init__(self, send_sem, recv_sem, local_sem):
        self.send_sem, self.recv_sem, self.local_sem = send_sem, recv_sem, local_sem
        self.sent, self.local, self.kept = [], [], 0
        f, e = lax.axis_index("fsdp"), lax.axis_index("expert")
        self.y, self.c = f // 2, lax.rem(f, 2)
        self.z, self.x = e // 4, lax.rem(e, 4)

    def place(self, axis):
        return {"x": self.x, "y": self.y, "z": self.z}[axis]

    def device(self, axis, d):
        y, c, z, x = self.y, self.c, self.z, self.x
        if axis == "core":
            c = 1 - c
        elif axis == "y":
            y = around(y, d)
        elif axis == "z":
            z = around(z, d)
        elif axis == "x":
            x = around(x, d)
        return (y * 2 + c, z * 4 + x)

    def greet(self, axes, group=False):
        barrier = pltpu.get_barrier_semaphore()
        partners = []
        for axis in axes:
            for d in (1,) if axis == "core" else (1, -1):
                partners.append(self.device(axis, d))
        for partner in partners:
            pl.semaphore_signal(barrier, inc=1, device_id=partner, device_id_type=MESH)
        count = len(partners)
        if group:
            e = self.z * 4 + self.x
            for i in range(1, 16):
                pl.semaphore_signal(
                    barrier,
                    inc=1,
                    device_id=(self.y * 2 + self.c, lax.rem(e + i, 16)),
                    device_id_type=MESH,
                )
            count += 15
        pl.semaphore_wait(barrier, count)

    def send(self, src, dst, device, land):
        k = len(self.sent)
        copy = pltpu.make_async_remote_copy(
            src, dst, self.send_sem.at[k], self.recv_sem.at[k], device_id=device, device_id_type=MESH
        )
        copy.start()
        arriving = pltpu.make_async_remote_copy(
            land, land, self.send_sem.at[k], self.recv_sem.at[k], device_id=device, device_id_type=MESH
        )
        self.sent.append(copy)
        return Event(copy, arriving)

    def keep(self, src, dst):
        copy = pltpu.make_async_copy(src, dst, self.local_sem.at[self.kept])
        copy.start()
        self.local.append(copy)
        self.kept += 1

    def settle(self):
        for copy in self.local:
            copy.wait()
        self.local = []

    def finish(self):
        for copy in self.sent:
            copy.wait_send()
        self.settle()


def around(p, d):
    return lax.rem(p + (d + 4), 4)


def in_turn(steps):
    queue = []
    for n, step in enumerate(steps):
        due = next(step, None)
        if due is not None:
            queue.append((due, n))
    while queue:
        queue.sort()
        _, n = queue.pop(0)
        due = next(steps[n], None)
        if due is not None:
            queue.append((due, n))


def us(count):
    return count * 2 / 50e3


def gather_pack(net, inp, out, view, start, size, total):
    y, c = net.y, net.c
    slot = lambda d, core: around(y, d) * 2 + core
    here = lambda d, half=None: view(out, slot(d, c), half)
    there = lambda d, half=None: view(out, slot(d, 1 - c), half)
    right, left, mate = net.device("y", 1), net.device("y", -1), net.device("core", 0)
    to_right = net.send(inp, here(0), right, here(-1))
    to_left = net.send(inp, here(0), left, here(1))
    over = [net.send(inp, here(0), mate, there(0))]
    net.keep(inp, here(0))
    yield 1 + start + size
    to_right.arrived()
    far0 = net.send(here(-1, 0), here(-1, 0), right, here(2, 0))
    over.append(net.send(here(-1), here(-1), mate, there(-1)))
    to_left.arrived()
    far1 = net.send(here(1, 1), here(1, 1), left, here(2, 1))
    over.append(net.send(here(1), here(1), mate, there(1)))
    yield 2 + total + (start + size) / 2
    far0.arrived()
    over.append(net.send(here(2, 0), here(2, 0), mate, there(2, 0)))
    far1.arrived()
    over.append(net.send(here(2, 1), here(2, 1), mate, there(2, 1)))
    yield 1000
    for event in over:
        event.arrived()


def gather_plane(net, inp, out, view, part, start, u):
    one, two = ("x", "z") if part == 0 else ("z", "x")
    p, q = net.place(one), net.place(two)

    def slot(dp, dq):
        a, b = around(p, dp), around(q, dq)
        return b * 4 + a if part == 0 else a * 4 + b

    at = lambda dp, dq, half=None: view(out, slot(dp, dq), part, half)
    own = view(inp, None, part, None)
    right1, left1 = net.device(one, 1), net.device(one, -1)
    right2, left2 = net.device(two, 1), net.device(two, -1)
    to_right = net.send(own, at(0, 0), right1, at(-1, 0))
    to_left = net.send(own, at(0, 0), left1, at(1, 0))

    def spread(dp):
        src = own if dp == 0 else at(dp, 0)
        return (
            dp,
            net.send(src, at(dp, 0), right2, at(dp, -1)),
            net.send(src, at(dp, 0), left2, at(dp, 1)),
        )

    spreads = [spread(0)]
    net.keep(own, at(0, 0))
    yield start + 1 + u
    to_right.arrived()
    far0 = net.send(at(-1, 0, 0), at(-1, 0, 0), right1, at(2, 0, 0))
    spreads.append(spread(-1))
    to_left.arrived()
    far1 = net.send(at(1, 0, 1), at(1, 0, 1), left1, at(2, 0, 1))
    spreads.append(spread(1))
    yield start + 2 + 2 * u
    last = []

    def relay(item):
        dp, from_left, from_right = item
        from_left.arrived()
        last.append(net.send(at(dp, -1, 0), at(dp, -1, 0), right2, at(dp, 2, 0)))
        from_right.arrived()
        last.append(net.send(at(dp, 1, 1), at(dp, 1, 1), left2, at(dp, 2, 1)))

    relay(spreads[0])
    yield start + 2.5 + 2.5 * u
    far0.arrived()
    far1.arrived()
    spreads.append(spread(2))
    yield start + 3 + 3.5 * u
    relay(spreads[1])
    yield start + 3 + 4.5 * u
    relay(spreads[2])
    yield start + 4 + 6 * u
    relay(spreads[3])
    yield 1000
    for event in last:
        event.arrived()


def plain(ref):
    return ref[...].astype(F32)


class Ring:
    def __init__(self, net, axis, source, own, put, landing, sums):
        self.net, self.source, self.own, self.put = net, source, own, put
        self.landing, self.sums = landing, sums
        self.right, self.left = net.device(axis, 1), net.device(axis, -1)

    def go(self, n, src, device):
        return self.net.send(src, self.landing.at[n], device, self.landing.at[n])

    def far(self):
        self.far_right = self.go(0, self.source(2, 0), self.right)
        self.far_left = self.go(1, self.source(2, 1), self.left)

    def near_right(self):
        self.from_left = self.go(2, self.source(1, 1), self.right)

    def near_left(self):
        self.from_right = self.go(3, self.source(-1, 0), self.left)

    def relay(self):
        self.far_right.arrived()
        self.sums[0] = (plain(self.source(1, 0)) + plain(self.landing.at[0])).astype(BF)
        self.sum_right = self.go(4, self.sums.at[0], self.right)
        self.far_left.arrived()
        self.sums[1] = (plain(self.source(-1, 1)) + plain(self.landing.at[1])).astype(BF)
        self.sum_left = self.go(5, self.sums.at[1], self.left)

    def close(self):
        self.from_right.arrived()
        self.sum_right.arrived()
        self.put(0, self.own(0) + plain(self.landing.at[3]) + plain(self.landing.at[4]))
        self.from_left.arrived()
        self.sum_left.arrived()
        self.put(1, self.own(1) + plain(self.landing.at[2]) + plain(self.landing.at[5]))


def sum_plane(net, part, payload, cols, put, landing, sums, accs):
    one, two = ("z", "x") if part == 0 else ("x", "z")
    p, q = net.place(one), net.place(two)
    columns = pl.ds(part * cols, cols)
    half_rows = payload.shape[1] // 2
    u = us(payload.shape[1] * cols)

    def slot(dp, dq):
        a, b = around(p, dp), around(q, dq)
        return a * 4 + b if part == 0 else b * 4 + a

    rings = []
    for n, dq in enumerate((2, 1, -1, 0)):

        def source(d, half, dq=dq):
            return payload.at[slot(d, dq), pl.ds(half * half_rows, half_rows), columns]

        def own(half, source=source):
            return plain(source(0, half))

        def keep(half, value, n=n):
            accs[n, half] = value.astype(BF)

        rings.append(Ring(net, one, source, own, keep, landing.at[n], sums.at[n]))
    at = {2: 0, 1: 1, -1: 2, 0: 3}
    last = Ring(
        net,
        two,
        lambda d, half: accs.at[at[d], half],
        lambda half: plain(accs.at[3, half]),
        put,
        landing.at[4],
        sums.at[4],
    )
    for ring in rings:
        ring.far()
    for ring in rings:
        ring.near_right()
        ring.near_left()
    for n in range(4):
        yield 2 + 0.5 * (n + 1) * u
        rings[n].relay()
    for n in range(4):
        yield 3 + (4 + 0.5 * (n + 1)) * u
        rings[n].close()
        if n == 0:
            last.far()
        elif n == 1:
            last.near_right()
        elif n == 2:
            last.near_left()
    yield 4 + 6.5 * u
    last.relay()
    yield 6 + 7.5 * u
    last.close()


def sum_pack(net, payload, view, put, start, b, pairs, landing, sums):
    y, c = net.y, net.c
    mate = net.device("core", 0)
    order = (2, 1, -1, 0)
    slot = lambda d, core: around(y, d) * 2 + core
    events = [
        net.send(view(payload, slot(d, 1 - c)), pairs.at[n], mate, pairs.at[n])
        for n, d in enumerate(order)
    ]
    at = {2: 0, 1: 1, -1: 2}
    source = lambda d, half: pairs.at[at[d], half]
    own = lambda half: plain(view(payload, slot(0, c)).at[half]) + plain(pairs.at[3, half])
    ring = Ring(net, "y", source, own, put, landing, sums)

    def both(n):
        events[n].arrived()
        for half in range(2):
            pairs[n, half] = (
                plain(view(payload, slot(order[n], c)).at[half]) + plain(pairs.at[n, half])
            ).astype(BF)

    yield 1 + start / 5
    both(0)
    ring.far()
    yield 1 + start / 5 + b / 10
    both(1)
    ring.near_right()
    both(2)
    ring.near_left()
    yield 2 + start + b * 0.6
    ring.relay()
    yield 3 + start + b * 1.5
    events[3].arrived()
    ring.close()


def sum_all(net, part, whole, out, now, landing1, sums1, accs, landing2, sums2, blocks):
    one, two = ("x", "z") if part == 0 else ("z", "x")
    p, q = net.place(one), net.place(two)
    wide = whole.shape[3] // 4

    def keep(half, value):
        for b in range(4):
            accs[b, half] = value[:, b * wide : (b + 1) * wide].astype(BF)

    def block(half, value):
        blocks[q, half] = value.astype(BF)

    ring = Ring(
        net,
        one,
        lambda d, half: whole.at[around(p, d), half],
        lambda half: plain(whole.at[p, half]),
        keep,
        landing1,
        sums1,
    )
    then = Ring(
        net,
        two,
        lambda d, half: accs.at[around(q, d), half],
        lambda half: plain(accs.at[q, half]),
        block,
        landing2,
        sums2,
    )
    for r in (ring, then):
        r.far()
        r.near_right()
        r.near_left()
        now += 2.5
        yield now
        r.relay()
        now += 2.5
        yield now
        r.close()
    for due in ring_gather(net, two, blocks):
        yield now + due
    now += 5
    for b in range(4):
        for half in range(2):
            out[p, half, :, b * wide : (b + 1) * wide] = blocks[b, half]
    for due in ring_gather(net, one, out):
        yield now + due


def ring_gather(net, axis, ref):
    p = net.place(axis)
    right, left = net.device(axis, 1), net.device(axis, -1)
    at = lambda d: ref.at[around(p, d)]
    to_right = net.send(at(0), at(0), right, at(-1))
    to_left = net.send(at(0), at(0), left, at(1))
    yield 2.5
    to_right.arrived()
    far0 = net.send(at(-1).at[0], at(-1).at[0], right, at(2).at[0])
    to_left.arrived()
    far1 = net.send(at(1).at[1], at(1).at[1], left, at(2).at[1])
    yield 5
    far0.arrived()
    far1.arrived()


def swap_small(net, payload, out):
    e = net.z * 4 + net.x
    f = net.y * 2 + net.c
    events = []
    for i in range(1, 16):
        to, source = lax.rem(e + i, 16), lax.rem(e + (16 - i), 16)
        events.append(net.send(payload.at[to], out.at[e], (f, to), out.at[source]))
    net.keep(payload.at[e], out.at[e])
    yield 1000
    for event in events:
        event.arrived()


ANY = pl.BlockSpec(memory_space=pl.ANY)
INSIDE = pl.BlockSpec(memory_space=pltpu.VMEM)


def call(kernel, ident, ins, outs, in_space, out_space, scratch, events, keeps):
    return pl.pallas_call(
        kernel,
        out_shape=outs,
        in_specs=in_space,
        out_specs=out_space,
        scratch_shapes=[
            *scratch,
            pltpu.SemaphoreType.DMA((events,)),
            pltpu.SemaphoreType.DMA((events,)),
            pltpu.SemaphoreType.DMA((max(keeps, 1),)),
        ],
        compiler_params=pltpu.CompilerParams(
            collective_id=ident, has_side_effects=True, vmem_limit_bytes=56 << 20
        ),
    )(*ins)


def rows_view(ref, slot, half):
    rows = ref.shape[1]
    if half is None:
        return ref.at[slot]
    return ref.at[slot, pl.ds(half * (rows // 2), rows // 2)]


def pair_view(ref, slot, half):
    if half is None:
        return ref.at[:, slot]
    return ref.at[half, slot]


def plane_view(ref, slot, part, half):
    rows, cols = ref.shape[-2] // 2, ref.shape[-1] // 2
    where = () if slot is None else (slot,)
    if half is None:
        return ref.at[(*where, slice(None), pl.ds(part * cols, cols))]
    return ref.at[(*where, pl.ds(half * rows, rows), pl.ds(part * cols, cols))]


def quarter_view(ref, slot, part, half):
    where = () if slot is None else (slot,)
    if half is None:
        return ref.at[(*where, pl.ds(part * 2, 2))]
    return ref.at[(*where, part * 2 + half)]


def gather_kernel(views, planes, *refs):
    packs = len(views)
    total = packs + planes
    ins, outs = refs[:total], refs[total : 2 * total]
    net = Net(*refs[2 * total :])
    net.greet((["core", "y"] if packs else []) + (["x", "z"] if planes else []))
    steps, start = [], 0.0
    for i in range(planes):
        inp, out = ins[packs + i], outs[packs + i]
        u = us(inp.shape[0] * inp.shape[1] // 2)
        for part in range(2):
            steps.append(gather_plane(net, inp, out, plane_view, part, start, u))
        start += u / 2
    sizes = [us(functools.reduce(lambda a, b: a * b, r.shape)) for r in ins[:packs]]
    start = 0.0
    for i in range(packs):
        steps.append(gather_pack(net, ins[i], outs[i], views[i], start, sizes[i], sum(sizes)))
        start += sizes[i]
    in_turn(steps)
    net.finish()


def gather(ident, pack_arrays, plane_arrays):
    views, outs = [], []
    for a in pack_arrays:
        if a.ndim == 2:
            views.append(rows_view)
            outs.append(jax.ShapeDtypeStruct((8, *a.shape), a.dtype))
        else:
            views.append(pair_view)
            outs.append(jax.ShapeDtypeStruct((a.shape[0], 8, *a.shape[1:]), a.dtype))
    for a in plane_arrays:
        outs.append(jax.ShapeDtypeStruct((16, *a.shape), a.dtype))
    n, m = len(pack_arrays), len(plane_arrays)
    result = call(
        functools.partial(gather_kernel, tuple(views), m),
        ident,
        [*pack_arrays, *plane_arrays],
        outs,
        [ANY] * (n + m),
        [ANY] * (n + m),
        [],
        9 * n + 40 * m,
        n + 2 * m,
    )
    packed = []
    for a, r in zip(pack_arrays, result[:n]):
        if a.ndim == 2:
            packed.append(r.reshape(8 * a.shape[0], a.shape[1]))
        else:
            packed.append(r.reshape(a.shape[0], 8 * a.shape[1], a.shape[2]))
    return packed, result[n:]


def put_into(ref):
    def put(half, value):
        ref[half] = value.astype(ref.dtype)

    return put


def block_view(ref, slot):
    return ref.at[slot]


def pair_block_view(ref, slot):
    return ref.at[:, slot]


def scatter_kernel(kinds, planes, swaps, finals, *refs):
    refs = list(refs)
    take = lambda n: [refs.pop(0) for _ in range(n)]
    packs = len(kinds)
    pack_in, plane_in, swap_in = take(packs), take(planes), take(swaps)
    pack_out, plane_out, swap_out = take(packs), take(planes), take(swaps)
    pack_scratch = [take(3) for _ in range(packs)]
    plane_scratch = [[take(3) for _ in range(2)] for _ in range(planes)]
    small = [finals and r.shape[-1] == 128 for r in pack_in]
    final_scratch = [take(2 if small[i] else 7) for i in range(packs)] if finals else []
    net = Net(*refs)
    wide = planes or swaps or finals
    net.greet((["core", "y"] if packs else []) + (["x", "z"] if wide else []), group=bool(swaps))
    steps = []
    for i in range(planes):
        for part in range(2):
            cols = WIDTH // 2

            def put(half, value, i=i, part=part, cols=cols):
                rows = plane_in[i].shape[1] // 2
                plane_out[i][
                    half * rows : (half + 1) * rows, part * cols : (part + 1) * cols
                ] = value.astype(plane_out[i].dtype)

            steps.append(sum_plane(net, part, plane_in[i], cols, put, *plane_scratch[i][part]))
    for i in range(swaps):
        steps.append(swap_small(net, swap_in[i], swap_out[i]))

    def dense(i, start, b):
        whole, rest = final_scratch[i][0], final_scratch[i][1:]

        def put(half, value):
            n = value.shape[-1]
            whole[half * 2 : half * 2 + 2] = value.reshape(2, 2, 16, n).astype(BF)

        yield from sum_pack(net, pack_in[i], kinds[i], put, start, b, *pack_scratch[i])
        yield from sum_all(net, i % 2, whole, pack_out[i], start + 1.5 * b + 3, *rest)

    def narrow(i, start, b):
        whole, landed = final_scratch[i]

        def put(half, value):
            whole[half * 2 : half * 2 + 2] = value.reshape(2, 32, 128).astype(BF)

        yield from sum_pack(net, pack_in[i], kinds[i], put, start, b, *pack_scratch[i])
        now = start + 1.5 * b + 3
        parts = [
            gather_plane(net, whole, landed, quarter_view, part, now, 1.0) for part in range(2)
        ]
        while parts:
            due = [next(p, None) for p in parts]
            if None in due:
                break
            yield max(due)
        net.settle()
        total = plain(landed.at[0])
        for n in range(1, 16):
            total = total + plain(landed.at[n])
        pack_out[i][...] = total

    start = 0.0
    for i in range(packs):
        values = functools.reduce(lambda a, b: a * b, pack_in[i].shape) // 8
        b = us(values)
        scratch = pack_scratch[i]
        if not finals:
            put = put_into(pack_out[i])
            steps.append(sum_pack(net, pack_in[i], kinds[i], put, start, b, *scratch))
        elif small[i]:
            steps.append(narrow(i, start, b))
        else:
            steps.append(dense(i, start, b))
        start += 1.5 * b
    in_turn(steps)
    net.finish()


def scatter(ident, pack_arrays, plane_arrays, swap_arrays=(), finals=False):
    kinds, outs, scratch, keeps = [], [], [], len(swap_arrays)
    for a in pack_arrays:
        if a.shape[0] == 2:
            kinds.append(pair_block_view)
            block = (2, *a.shape[2:])
        else:
            kinds.append(block_view)
            block = a.shape[1:]
        half = block[1:]
        if finals and block[-1] == 128:
            outs.append(jax.ShapeDtypeStruct((4, 32, 128), F32))
        elif finals:
            outs.append(jax.ShapeDtypeStruct((4, 2, 16, block[-1]), BF))
        else:
            outs.append(jax.ShapeDtypeStruct(block, BF))
        scratch += [
            pltpu.VMEM((4, *block), BF),
            pltpu.VMEM((6, *half), BF),
            pltpu.VMEM((2, *half), BF),
        ]
    for a in plane_arrays:
        rows, cols = a.shape[1] // 2, a.shape[2] // 2
        outs.append(jax.ShapeDtypeStruct(a.shape[1:], F32))
        for _ in range(2):
            scratch += [
                pltpu.VMEM((5, 6, rows, cols), BF),
                pltpu.VMEM((5, 2, rows, cols), BF),
                pltpu.VMEM((4, 2, rows, cols), BF),
            ]
    for a in swap_arrays:
        outs.append(jax.ShapeDtypeStruct(a.shape, a.dtype))
    events = 10 * len(pack_arrays) + 60 * len(plane_arrays) + 15 * len(swap_arrays)
    if finals:
        for a in pack_arrays:
            n = a.shape[-1]
            if n == 128:
                scratch += [pltpu.VMEM((4, 32, 128), BF), pltpu.VMEM((16, 4, 32, 128), BF)]
                events += 40
                keeps += 2
                continue
            scratch += [
                pltpu.VMEM((4, 2, 16, n), BF),
                pltpu.VMEM((6, 16, n), BF),
                pltpu.VMEM((2, 16, n), BF),
                pltpu.VMEM((4, 2, 16, n // 4), BF),
                pltpu.VMEM((6, 16, n // 4), BF),
                pltpu.VMEM((2, 16, n // 4), BF),
                pltpu.VMEM((4, 2, 16, n // 4), BF),
            ]
            events += 20
    ins = [*pack_arrays, *plane_arrays, *swap_arrays]
    return call(
        functools.partial(
            scatter_kernel, tuple(kinds), len(plane_arrays), len(swap_arrays), finals
        ),
        ident,
        ins,
        outs,
        [INSIDE] * len(ins),
        [INSIDE] * len(ins),
        scratch,
        events,
        keeps,
    )


KEYS = 8 * ROWS
BLOCK = 256
FOUR = 4 * ROWS


def dot_last(a, b):
    return lax.dot_general(a, b, (((1,), (1,)), ((), ())), preferred_element_type=F32)


def dot_first(a, b):
    return lax.dot_general(a, b, (((0,), (0,)), ((), ())), preferred_element_type=F32)


def low_lanes(rows):
    return lax.broadcasted_iota(jnp.int32, (rows, 128), 1) < HEAD_SIZE


def four_heads(v):
    low = low_lanes(ROWS)
    a, b = v[:, :128], v[:, 128:]
    zero = jnp.zeros_like(a)
    return jnp.concatenate(
        [
            jnp.where(low, a, zero),
            jnp.where(low, pltpu.roll(a, HEAD_SIZE, 1), zero),
            jnp.where(low, zero, pltpu.roll(b, HEAD_SIZE, 1)),
            jnp.where(low, zero, b),
        ],
        axis=0,
    )


def side_by_side(v):
    low = low_lanes(ROWS)
    r = [v[i * ROWS : (i + 1) * ROWS] for i in range(4)]
    return jnp.concatenate(
        [
            jnp.where(low, r[0], pltpu.roll(r[1], HEAD_SIZE, 1)),
            jnp.where(low, pltpu.roll(r[2], HEAD_SIZE, 1), r[3]),
        ],
        axis=1,
    )


def set_bias(span_ref, bias):
    @pl.when(pl.program_id(0) == 0)
    def _():
        first, last = span_ref[0:1, :], span_ref[1:2, :]
        for b in range(0, KEYS, BLOCK):
            at = lax.broadcasted_iota(jnp.int32, (BLOCK, FOUR), 0) + b
            bias[b : b + BLOCK] = jnp.where((at >= first) & (at <= last), 0.0, -1e30)


def attend_kernel(q_ref, k_ref, v_ref, span_ref, o_ref, lse_ref, bias, score):
    set_bias(span_ref, bias)
    q = four_heads(q_ref[...].astype(F32) * HEAD_SIZE ** (-0.5)).astype(BF)
    top = jnp.full((1, FOUR), -3e38, F32)
    for b in range(0, KEYS, BLOCK):
        s = dot_last(k_ref[b : b + BLOCK], q) + bias[b : b + BLOCK]
        score[b : b + BLOCK] = s
        top = jnp.maximum(top, jnp.max(s, axis=0, keepdims=True))
    total = jnp.zeros((1, FOUR), F32)
    out = jnp.zeros((128, FOUR), F32)
    for b in range(0, KEYS, BLOCK):
        e = jnp.exp(score[b : b + BLOCK] - top)
        total = total + jnp.sum(e, axis=0, keepdims=True)
        out = out + dot_first(v_ref[b : b + BLOCK], e.astype(BF))
    o_ref[...] = side_by_side((out / total).T).astype(BF)
    lse_ref[0] = jnp.broadcast_to(top + jnp.log(total), (8, FOUR))


def attend(query, kv, span):
    return pl.pallas_call(
        attend_kernel,
        grid=(4,),
        in_specs=[
            pl.BlockSpec((ROWS, 256), lambda p: (0, p)),
            pl.BlockSpec((KEYS, 128), lambda p: (0, p)),
            pl.BlockSpec((KEYS, 128), lambda p: (0, 4 + p)),
            pl.BlockSpec((8, FOUR), lambda p: (0, 0)),
        ],
        out_specs=[
            pl.BlockSpec((ROWS, 256), lambda p: (0, p)),
            pl.BlockSpec((1, 8, FOUR), lambda p: (p, 0, 0)),
        ],
        out_shape=[
            jax.ShapeDtypeStruct((ROWS, WIDTH), BF),
            jax.ShapeDtypeStruct((4, 8, FOUR), F32),
        ],
        scratch_shapes=[pltpu.VMEM((KEYS, FOUR), F32), pltpu.VMEM((KEYS, FOUR), F32)],
        compiler_params=pltpu.CompilerParams(vmem_limit_bytes=48 << 20),
    )(query, kv, kv, span)


def attend_back_kernel(
    q_ref, k_ref, v_ref, g_ref, o_ref, lse_ref, span_ref, dq_ref, dk_ref, dv_ref, bias
):
    set_bias(span_ref, bias)
    q = four_heads(q_ref[...].astype(F32) * HEAD_SIZE ** (-0.5)).astype(BF)
    wide = four_heads(g_ref[...].astype(F32))
    g = wide.astype(BF)
    spread = jnp.sum((wide * four_heads(o_ref[...].astype(F32))).T, axis=0, keepdims=True)
    lse = lse_ref[0, 0:1, :]
    dq = jnp.zeros((128, FOUR), F32)
    for b in range(0, KEYS, BLOCK):
        k = k_ref[b : b + BLOCK]
        p = jnp.exp(dot_last(k, q) + bias[b : b + BLOCK] - lse)
        dp = dot_last(v_ref[b : b + BLOCK], g)
        ds = (p * (dp - spread)).astype(BF)
        dv_ref[b : b + BLOCK] = jnp.dot(p.astype(BF), g, preferred_element_type=F32).astype(BF)
        dk_ref[b : b + BLOCK] = jnp.dot(ds, q, preferred_element_type=F32).astype(BF)
        dq = dq + dot_first(k, ds)
    dq_ref[...] = side_by_side(dq.T * HEAD_SIZE ** (-0.5))


def attend_back(query, kv, grad, attended, lse, span):
    return pl.pallas_call(
        attend_back_kernel,
        grid=(4,),
        in_specs=[
            pl.BlockSpec((ROWS, 256), lambda p: (0, p)),
            pl.BlockSpec((KEYS, 128), lambda p: (0, p)),
            pl.BlockSpec((KEYS, 128), lambda p: (0, 4 + p)),
            pl.BlockSpec((ROWS, 256), lambda p: (0, p)),
            pl.BlockSpec((ROWS, 256), lambda p: (0, p)),
            pl.BlockSpec((1, 8, FOUR), lambda p: (p, 0, 0)),
            pl.BlockSpec((8, FOUR), lambda p: (0, 0)),
        ],
        out_specs=[
            pl.BlockSpec((ROWS, 256), lambda p: (0, p)),
            pl.BlockSpec((KEYS, 128), lambda p: (0, p)),
            pl.BlockSpec((KEYS, 128), lambda p: (0, p)),
        ],
        out_shape=[
            jax.ShapeDtypeStruct((ROWS, WIDTH), F32),
            jax.ShapeDtypeStruct((KEYS, 512), BF),
            jax.ShapeDtypeStruct((KEYS, 512), BF),
        ],
        scratch_shapes=[pltpu.VMEM((KEYS, FOUR), F32)],
        compiler_params=pltpu.CompilerParams(vmem_limit_bytes=48 << 20),
    )(query, kv, kv, grad, attended, lse, span)


def contract_first(left_op, right_op):
    return lax.dot_general(left_op, right_op, (((0,), (0,)), ((), ())), preferred_element_type=F32)


def contract_last(left_op, right_op):
    return lax.dot_general(left_op, right_op, (((1,), (1,)), ((), ())), preferred_element_type=F32)


def rotary(offset, width):
    half_dim = HEAD_SIZE // 2
    lane = jnp.arange(width, dtype=jnp.int32)
    frequency = BASE ** (-2.0 * (lane % half_dim).astype(F32) / HEAD_SIZE)
    angles = offset.astype(F32)[:, None] * frequency[None, :]
    return jnp.cos(angles), jnp.sin(angles)


def swapped(v):
    half_dim = HEAD_SIZE // 2
    first = (jnp.arange(v.shape[1], dtype=jnp.int32) % HEAD_SIZE < half_dim)[None, :]
    return jnp.where(first, -jnp.roll(v, -half_dim, axis=1), jnp.roll(v, half_dim, axis=1))


def norm_back(inputs, inverse_rms, gain_vec, upstream):
    scaled = upstream * gain_vec
    gain_grad = jnp.sum(upstream * inputs * inverse_rms, axis=0)
    spread = jnp.mean(scaled * inputs, axis=-1, keepdims=True)
    return (inverse_rms * scaled - inputs * inverse_rms**3 * spread, gain_grad)


def mm(pattern, a, b):
    return jnp.einsum(pattern, a, b, preferred_element_type=F32)


def shards(
    hidden_in,
    grad_out,
    lengths,
    experts,
    gain_attn,
    w_query,
    key_weight,
    value_weight,
    w_out,
    gain_moe,
    w_router,
    expert_gate,
    expert_up,
    expert_down,
):
    fsdp = lax.axis_index("fsdp")
    owner = lax.axis_index("expert")
    inputs = hidden_in[0].astype(F32)
    upstream = grad_out[0].astype(F32)
    picked = experts[0]

    named = jnp.any(
        picked[None, :, :] == jnp.arange(EXPERTS, dtype=jnp.int32)[:, None, None], axis=-1
    )
    named_wide = jnp.pad(named.astype(BF), ((0, 0), (0, LANES - ROWS)))
    small = jnp.concatenate(
        [w_router, gain_attn[:, None], gain_moe[:, None], jnp.zeros((128, 94), BF)], axis=1
    )
    (full_query, full_key, full_value, full_out, full_small), (all_up, all_named) = gather(
        0, [w_query, key_weight, value_weight, w_out, small], [grad_out[0], named_wide]
    )
    full_router = full_small[:, :EXPERTS]
    full_gain_a = full_small[:, EXPERTS].astype(F32)
    full_gain_m = full_small[:, EXPERTS + 1].astype(F32)

    seq_lengths = lengths[0]
    seq_ends = jnp.cumsum(seq_lengths, dtype=jnp.int32)
    starts = seq_ends - seq_lengths

    def places(index):
        inside = (index[:, None] >= starts[None, :]) & (index[:, None] < seq_ends[None, :])
        inside = inside.astype(jnp.int32)
        return jnp.sum(inside * (index[:, None] - starts[None, :]), axis=1)

    own_index = fsdp * ROWS + jnp.arange(ROWS, dtype=jnp.int32)
    own_offset = places(own_index)
    cosine, sine = rotary(own_offset, WIDTH)
    cosine_k, sine_k = cosine[:, :512], sine[:, :512]
    span = jnp.concatenate(
        [
            jnp.tile(own_index - own_offset, 4)[None, :],
            jnp.tile(own_index, 4)[None, :],
            jnp.zeros((6, FOUR), jnp.int32),
        ]
    )

    inverse_a = lax.rsqrt(jnp.mean(inputs * inputs, axis=-1, keepdims=True) + EPS)
    normed = (inputs * inverse_a * full_gain_a).astype(BF)
    query = jnp.dot(normed, full_query, preferred_element_type=F32)
    key = jnp.dot(normed, full_key, preferred_element_type=F32)
    value = jnp.dot(normed, full_value, preferred_element_type=F32).astype(BF)
    query = (query * cosine + swapped(query) * sine).astype(BF)
    key = (key * cosine_k + swapped(key) * sine_k).astype(BF)
    (kv,), _ = gather(1, [jnp.concatenate([key, value], axis=1)], [])
    attended, lse = attend(query, kv, span)
    hidden = inputs + jnp.dot(attended, full_out, preferred_element_type=F32)
    inverse_m = lax.rsqrt(jnp.mean(hidden * hidden, axis=-1, keepdims=True) + EPS)
    routed = (hidden * inverse_m * full_gain_m).astype(BF)

    (full_gate, full_up, full_down), (all_routed,) = gather(
        2, [expert_gate, expert_up, expert_down], [routed]
    )
    all_named = all_named[:, :, :ROWS]
    logits = mm("de,std->set", full_router, all_routed)
    logits = jnp.where(all_named > 0, logits, -1e30)
    own_logits = lax.dynamic_slice_in_dim(logits, 2 * owner, 2, axis=1)
    own_named = lax.dynamic_slice_in_dim(all_named, 2 * owner, 2, axis=1)
    top = jnp.max(logits, axis=1, keepdims=True)
    total = jnp.sum(jnp.exp(logits - top), axis=1, keepdims=True)
    own_gates = jnp.exp(own_logits - top) / total * own_named.astype(F32)
    before = (
        jnp.arange(ROWS, dtype=jnp.int32)[:, None] < jnp.arange(ROWS, dtype=jnp.int32)[None, :]
    ).astype(BF)
    rank = mm("sjt,tu->sju", own_named, before).astype(jnp.int32)
    pick = (
        (rank[:, :, None, :] == jnp.arange(SLOTS, dtype=jnp.int32)[None, None, :, None])
        & (own_named[:, :, None, :] > 0)
    ).astype(BF)
    slot_gates = jnp.sum(pick.astype(F32) * own_gates[:, :, None, :], axis=-1)
    taken = mm("sjct,std->jscd", pick, all_routed).astype(BF).reshape(2, 16 * SLOTS, WIDTH)
    taken_up = mm("sjct,std->jscd", pick, all_up).astype(BF).reshape(2, 16 * SLOTS, WIDTH)
    slot_gates = slot_gates.transpose(1, 0, 2).reshape(2, 16 * SLOTS, 1)
    gate_part = mm("jrd,jdf->jrf", taken, full_gate)
    up_part = mm("jrd,jdf->jrf", taken, full_up)
    sigmoid_gate = jax.nn.sigmoid(gate_part)
    inner = (gate_part * sigmoid_gate * up_part).astype(BF)
    produced = mm("jrf,jfd->jrd", inner, full_down).astype(BF).astype(F32)
    up_rows = taken_up.astype(F32)
    gate_dots = jnp.sum(produced * up_rows, axis=-1).reshape(2, 16, SLOTS)
    weighed = (slot_gates * produced).astype(BF).reshape(2, 16, SLOTS, WIDTH)
    grad_rows = (slot_gates * up_rows).astype(BF)
    part_out = mm("sjct,jscd->std", pick, weighed).astype(BF)
    grad_inner = mm("jrd,jfd->jrf", grad_rows, full_down)
    grad_gate_part = (
        grad_inner * up_part * sigmoid_gate * (1.0 + gate_part * (1.0 - sigmoid_gate))
    ).astype(BF)
    grad_up_part = (grad_inner * gate_part * sigmoid_gate).astype(BF)
    grad_taken = (
        mm("jrf,jdf->jrd", grad_gate_part, full_gate) + mm("jrf,jdf->jrd", grad_up_part, full_up)
    ).astype(BF)
    part_grad = mm("sjct,jscd->std", pick, grad_taken.reshape(2, 16, SLOTS, WIDTH)).astype(BF)
    grad_down_w = mm("jrf,jrd->jfd", inner, grad_rows).astype(BF)
    grad_gate_w = mm("jrd,jrf->jdf", taken, grad_gate_part).astype(BF)
    grad_up_w = mm("jrd,jrf->jdf", taken, grad_up_part).astype(BF)
    token_dots = jnp.sum(pick.astype(F32) * gate_dots.transpose(1, 0, 2)[:, :, :, None], axis=2)
    token_dots = jnp.pad(token_dots, ((0, 0), (0, 6), (0, LANES - ROWS)))
    sum_gate, sum_up, sum_down, grad_routed, dots = scatter(
        3,
        [
            grad_gate_w.reshape(2, 8, 128, 512),
            grad_up_w.reshape(2, 8, 128, 512),
            grad_down_w.reshape(2, 8, 64, 1024),
        ],
        [part_grad],
        [token_dots],
    )

    dots = dots[:, :2, :ROWS].reshape(EXPERTS, ROWS)
    here = jnp.where(named, contract_last(full_router.T, routed), -1e30)
    here = jnp.exp(here - jnp.max(here, axis=0, keepdims=True)) * named.astype(F32)
    gates = here / jnp.sum(here, axis=0, keepdims=True)
    grad_logits = (gates * (dots - jnp.sum(gates * dots, axis=0, keepdims=True))).astype(BF)
    grad_routed = grad_routed + mm("et,de->td", grad_logits, full_router)
    grad_router_w = mm("td,et->de", routed, grad_logits)
    grad_middle, grad_gain_m = norm_back(hidden, inverse_m, full_gain_m, grad_routed)
    grad_hidden = upstream + grad_middle
    grad_hidden_low = grad_hidden.astype(BF)
    grad_out_w = contract_first(attended, grad_hidden_low)
    grad_attended = contract_last(grad_hidden_low, full_out).astype(BF)
    grad_query, grad_key, grad_value = attend_back(query, kv, grad_attended, attended, lse, span)
    grad_key, grad_value = scatter(
        4, [grad_key.reshape(8, 2, 80, 512), grad_value.reshape(8, 2, 80, 512)], []
    )
    grad_key = grad_key.reshape(ROWS, 512).astype(F32)
    grad_value = grad_value.reshape(ROWS, 512)
    grad_query = (grad_query * cosine - swapped(grad_query) * sine).astype(BF)
    grad_key = (grad_key * cosine_k - swapped(grad_key) * sine_k).astype(BF)
    grad_kv = jnp.concatenate([grad_key, grad_value], axis=1)
    grad_query_w = contract_first(normed, grad_query).astype(BF)
    grad_kv_w = contract_first(normed, grad_kv).astype(BF)
    grad_normed = (
        contract_last(grad_query, full_query)
        + contract_last(grad_key, full_key)
        + contract_last(grad_value, full_value)
    )
    grad_first, grad_gain_a = norm_back(inputs, inverse_a, full_gain_a, grad_normed)
    grad_input = (grad_hidden + grad_first).astype(BF)
    grad_small = jnp.concatenate(
        [
            grad_router_w.astype(BF),
            grad_gain_a.astype(BF)[:, None],
            grad_gain_m.astype(BF)[:, None],
            jnp.zeros((WIDTH, 128 - 34), BF),
        ],
        axis=1,
    )
    block = lambda a: a.reshape(8, 2, 64, a.shape[-1])
    tot_query, tot_out, tot_kv, tot_small, moe_out = scatter(
        5,
        [block(grad_query_w), block(grad_out_w.astype(BF)), block(grad_kv_w), block(grad_small)],
        [part_out],
        finals=True,
    )
    output = (hidden + moe_out).astype(BF)
    flat = lambda a: a.reshape(128, a.shape[-1]).astype(F32)
    tot_kv, tot_small = flat(tot_kv), flat(tot_small)
    return (
        output[None],
        grad_input[None],
        tot_small[:, EXPERTS],
        flat(tot_query),
        tot_kv[:, :512],
        tot_kv[:, 512:],
        flat(tot_out),
        tot_small[:, EXPERTS + 1],
        tot_small[:, :EXPERTS],
        sum_gate.astype(F32),
        sum_up.astype(F32),
        sum_down.astype(F32),
    )


def solution(mesh):
    token, matrix, stack = P("expert", "fsdp", None), P("fsdp", None), P("expert", "fsdp", None)
    return jax.shard_map(
        shards,
        mesh=mesh,
        in_specs=(
            token,
            token,
            P("expert", None),
            token,
            P("fsdp"),
            matrix,
            matrix,
            matrix,
            matrix,
            P("fsdp"),
            matrix,
            stack,
            stack,
            stack,
        ),
        out_specs=(
            token,
            token,
            P("fsdp"),
            matrix,
            matrix,
            matrix,
            matrix,
            P("fsdp"),
            matrix,
            stack,
            stack,
            stack,
        ),
        check_vma=False,
    )
```

```python
import functools

import jax
import jax.numpy as jnp
from jax import lax
from jax.experimental import pallas as pl
from jax.experimental.pallas import tpu as pltpu
from jax.sharding import PartitionSpec as P

MESH = pl.DeviceIdType.MESH
QUERY_HEADS = 16
KEY_VALUE_HEADS = 8
HEAD_SIZE = 64
TOPK = 8
EXPERTS = 32
ROWS = 160
SLOTS = 64
LANES = 256
WIDTH = 1024
EPS = 1e-06
BASE = 10000.0
BF = jnp.bfloat16
F32 = jnp.float32


class Event:
    def __init__(self, copy, arriving):
        self.copy, self.arriving = copy, arriving

    def arrived(self):
        self.arriving.wait_recv()


class Net:
    def __init__(self, send_sem, recv_sem, local_sem):
        self.send_sem, self.recv_sem, self.local_sem = send_sem, recv_sem, local_sem
        self.sent, self.local, self.kept = [], [], 0
        f, e = lax.axis_index("fsdp"), lax.axis_index("expert")
        self.y, self.c = f // 2, lax.rem(f, 2)
        self.z, self.x = e // 4, lax.rem(e, 4)

    def place(self, axis):
        return {"x": self.x, "y": self.y, "z": self.z}[axis]

    def device(self, axis, d):
        y, c, z, x = self.y, self.c, self.z, self.x
        if axis == "core":
            c = 1 - c
        elif axis == "y":
            y = around(y, d)
        elif axis == "z":
            z = around(z, d)
        elif axis == "x":
            x = around(x, d)
        return (y * 2 + c, z * 4 + x)

    def greet(self, axes, group=False):
        barrier = pltpu.get_barrier_semaphore()
        partners = []
        for axis in axes:
            for d in (1,) if axis == "core" else (1, -1):
                partners.append(self.device(axis, d))
        for partner in partners:
            pl.semaphore_signal(barrier, inc=1, device_id=partner, device_id_type=MESH)
        count = len(partners)
        if group:
            e = self.z * 4 + self.x
            for i in range(1, 16):
                pl.semaphore_signal(
                    barrier,
                    inc=1,
                    device_id=(self.y * 2 + self.c, lax.rem(e + i, 16)),
                    device_id_type=MESH,
                )
            count += 15
        pl.semaphore_wait(barrier, count)

    def send(self, src, dst, device, land):
        k = len(self.sent)
        copy = pltpu.make_async_remote_copy(
            src, dst, self.send_sem.at[k], self.recv_sem.at[k], device_id=device, device_id_type=MESH
        )
        copy.start()
        arriving = pltpu.make_async_remote_copy(
            land, land, self.send_sem.at[k], self.recv_sem.at[k], device_id=device, device_id_type=MESH
        )
        self.sent.append(copy)
        return Event(copy, arriving)

    def keep(self, src, dst):
        copy = pltpu.make_async_copy(src, dst, self.local_sem.at[self.kept])
        copy.start()
        self.local.append(copy)
        self.kept += 1

    def settle(self):
        for copy in self.local:
            copy.wait()
        self.local = []

    def finish(self):
        for copy in self.sent:
            copy.wait_send()
        self.settle()


def around(p, d):
    return lax.rem(p + (d + 4), 4)


def in_turn(steps):
    queue = []
    for n, step in enumerate(steps):
        due = next(step, None)
        if due is not None:
            queue.append((due, n))
    while queue:
        queue.sort()
        _, n = queue.pop(0)
        due = next(steps[n], None)
        if due is not None:
            queue.append((due, n))


def us(count):
    return count * 2 / 50e3


def gather_pack(net, inp, out, view, start, size, total):
    y, c = net.y, net.c
    slot = lambda d, core: around(y, d) * 2 + core
    here = lambda d, half=None: view(out, slot(d, c), half)
    there = lambda d, half=None: view(out, slot(d, 1 - c), half)
    right, left, mate = net.device("y", 1), net.device("y", -1), net.device("core", 0)
    to_right = net.send(inp, here(0), right, here(-1))
    to_left = net.send(inp, here(0), left, here(1))
    over = [net.send(inp, here(0), mate, there(0))]
    net.keep(inp, here(0))
    yield 1 + start + size
    to_right.arrived()
    far0 = net.send(here(-1, 0), here(-1, 0), right, here(2, 0))
    over.append(net.send(here(-1), here(-1), mate, there(-1)))
    to_left.arrived()
    far1 = net.send(here(1, 1), here(1, 1), left, here(2, 1))
    over.append(net.send(here(1), here(1), mate, there(1)))
    yield 2 + total + (start + size) / 2
    far0.arrived()
    over.append(net.send(here(2, 0), here(2, 0), mate, there(2, 0)))
    far1.arrived()
    over.append(net.send(here(2, 1), here(2, 1), mate, there(2, 1)))
    yield 1000
    for event in over:
        event.arrived()


def gather_plane(net, inp, out, view, part, start, u):
    one, two = ("x", "z") if part == 0 else ("z", "x")
    p, q = net.place(one), net.place(two)

    def slot(dp, dq):
        a, b = around(p, dp), around(q, dq)
        return b * 4 + a if part == 0 else a * 4 + b

    at = lambda dp, dq, half=None: view(out, slot(dp, dq), part, half)
    own = view(inp, None, part, None)
    right1, left1 = net.device(one, 1), net.device(one, -1)
    right2, left2 = net.device(two, 1), net.device(two, -1)
    to_right = net.send(own, at(0, 0), right1, at(-1, 0))
    to_left = net.send(own, at(0, 0), left1, at(1, 0))

    def spread(dp):
        src = own if dp == 0 else at(dp, 0)
        return (
            dp,
            net.send(src, at(dp, 0), right2, at(dp, -1)),
            net.send(src, at(dp, 0), left2, at(dp, 1)),
        )

    spreads = [spread(0)]
    net.keep(own, at(0, 0))
    yield start + 1 + u
    to_right.arrived()
    far0 = net.send(at(-1, 0, 0), at(-1, 0, 0), right1, at(2, 0, 0))
    spreads.append(spread(-1))
    to_left.arrived()
    far1 = net.send(at(1, 0, 1), at(1, 0, 1), left1, at(2, 0, 1))
    spreads.append(spread(1))
    yield start + 2 + 2 * u
    last = []

    def relay(item):
        dp, from_left, from_right = item
        from_left.arrived()
        last.append(net.send(at(dp, -1, 0), at(dp, -1, 0), right2, at(dp, 2, 0)))
        from_right.arrived()
        last.append(net.send(at(dp, 1, 1), at(dp, 1, 1), left2, at(dp, 2, 1)))

    relay(spreads[0])
    yield start + 2.5 + 2.5 * u
    far0.arrived()
    far1.arrived()
    spreads.append(spread(2))
    yield start + 3 + 3.5 * u
    relay(spreads[1])
    yield start + 3 + 4.5 * u
    relay(spreads[2])
    yield start + 4 + 6 * u
    relay(spreads[3])
    yield 1000
    for event in last:
        event.arrived()


def plain(ref):
    return ref[...].astype(F32)


class Ring:
    def __init__(self, net, axis, source, own, put, landing, sums):
        self.net, self.source, self.own, self.put = net, source, own, put
        self.landing, self.sums = landing, sums
        self.right, self.left = net.device(axis, 1), net.device(axis, -1)

    def go(self, n, src, device):
        return self.net.send(src, self.landing.at[n], device, self.landing.at[n])

    def far(self):
        self.far_right = self.go(0, self.source(2, 0), self.right)
        self.far_left = self.go(1, self.source(2, 1), self.left)

    def near_right(self):
        self.from_left = self.go(2, self.source(1, 1), self.right)

    def near_left(self):
        self.from_right = self.go(3, self.source(-1, 0), self.left)

    def relay(self):
        self.far_right.arrived()
        self.sums[0] = (plain(self.source(1, 0)) + plain(self.landing.at[0])).astype(BF)
        self.sum_right = self.go(4, self.sums.at[0], self.right)
        self.far_left.arrived()
        self.sums[1] = (plain(self.source(-1, 1)) + plain(self.landing.at[1])).astype(BF)
        self.sum_left = self.go(5, self.sums.at[1], self.left)

    def close(self):
        self.from_right.arrived()
        self.sum_right.arrived()
        self.put(0, self.own(0) + plain(self.landing.at[3]) + plain(self.landing.at[4]))
        self.from_left.arrived()
        self.sum_left.arrived()
        self.put(1, self.own(1) + plain(self.landing.at[2]) + plain(self.landing.at[5]))


def sum_plane(net, part, payload, cols, put, landing, sums, accs):
    one, two = ("z", "x") if part == 0 else ("x", "z")
    p, q = net.place(one), net.place(two)
    columns = pl.ds(part * cols, cols)
    half_rows = payload.shape[1] // 2
    u = us(payload.shape[1] * cols)

    def slot(dp, dq):
        a, b = around(p, dp), around(q, dq)
        return a * 4 + b if part == 0 else b * 4 + a

    rings = []
    for n, dq in enumerate((2, 1, -1, 0)):

        def source(d, half, dq=dq):
            return payload.at[slot(d, dq), pl.ds(half * half_rows, half_rows), columns]

        def own(half, source=source):
            return plain(source(0, half))

        def keep(half, value, n=n):
            accs[n, half] = value.astype(BF)

        rings.append(Ring(net, one, source, own, keep, landing.at[n], sums.at[n]))
    at = {2: 0, 1: 1, -1: 2, 0: 3}
    last = Ring(
        net,
        two,
        lambda d, half: accs.at[at[d], half],
        lambda half: plain(accs.at[3, half]),
        put,
        landing.at[4],
        sums.at[4],
    )
    for ring in rings:
        ring.far()
    for ring in rings:
        ring.near_right()
        ring.near_left()
    for n in range(4):
        yield 2 + 0.5 * (n + 1) * u
        rings[n].relay()
    for n in range(4):
        yield 3 + (4 + 0.5 * (n + 1)) * u
        rings[n].close()
        if n == 0:
            last.far()
        elif n == 1:
            last.near_right()
        elif n == 2:
            last.near_left()
    yield 4 + 6.5 * u
    last.relay()
    yield 6 + 7.5 * u
    last.close()


def sum_pack(net, payload, view, put, start, b, pairs, landing, sums):
    y, c = net.y, net.c
    mate = net.device("core", 0)
    order = (2, 1, -1, 0)
    slot = lambda d, core: around(y, d) * 2 + core
    events = [
        net.send(view(payload, slot(d, 1 - c)), pairs.at[n], mate, pairs.at[n])
        for n, d in enumerate(order)
    ]
    at = {2: 0, 1: 1, -1: 2}
    source = lambda d, half: pairs.at[at[d], half]
    own = lambda half: plain(view(payload, slot(0, c)).at[half]) + plain(pairs.at[3, half])
    ring = Ring(net, "y", source, own, put, landing, sums)

    def both(n):
        events[n].arrived()
        for half in range(2):
            pairs[n, half] = (
                plain(view(payload, slot(order[n], c)).at[half]) + plain(pairs.at[n, half])
            ).astype(BF)

    yield 1 + start / 5
    both(0)
    ring.far()
    yield 1 + start / 5 + b / 10
    both(1)
    ring.near_right()
    both(2)
    ring.near_left()
    yield 2 + start + b * 0.6
    ring.relay()
    yield 3 + start + b * 1.5
    events[3].arrived()
    ring.close()


def peers(net):
    e, f = net.z * 4 + net.x, net.y * 2 + net.c
    for i in range(1, 16):
        to = lax.rem(e + i, 16)
        yield (f, to), to, lax.rem(e + (16 - i), 16)


def sum_all(net, whole, out, now, landed):
    e = net.z * 4 + net.x
    events = [
        net.send(whole.at[to], landed.at[e], device, landed.at[source])
        for device, to, source in peers(net)
    ]
    yield now + 4
    for event in events:
        event.arrived()
    total = plain(whole.at[e])
    for _, to, _ in peers(net):
        total = total + plain(landed.at[to])
    out[e] = total.astype(out.dtype)
    events = [
        net.send(out.at[e], out.at[e], device, out.at[source]) for device, _, source in peers(net)
    ]
    yield now + 9
    for event in events:
        event.arrived()


def swap_small(net, payload, out):
    e = net.z * 4 + net.x
    f = net.y * 2 + net.c
    events = []
    for i in range(1, 16):
        to, source = lax.rem(e + i, 16), lax.rem(e + (16 - i), 16)
        events.append(net.send(payload.at[to], out.at[e], (f, to), out.at[source]))
    net.keep(payload.at[e], out.at[e])
    yield 1000
    for event in events:
        event.arrived()


ANY = pl.BlockSpec(memory_space=pl.ANY)
INSIDE = pl.BlockSpec(memory_space=pltpu.VMEM)


def call(kernel, ident, ins, outs, in_space, out_space, scratch, events, keeps):
    return pl.pallas_call(
        kernel,
        out_shape=outs,
        in_specs=in_space,
        out_specs=out_space,
        scratch_shapes=[
            *scratch,
            pltpu.SemaphoreType.DMA((events,)),
            pltpu.SemaphoreType.DMA((events,)),
            pltpu.SemaphoreType.DMA((max(keeps, 1),)),
        ],
        compiler_params=pltpu.CompilerParams(
            collective_id=ident, has_side_effects=True, vmem_limit_bytes=56 << 20
        ),
    )(*ins)


def rows_view(ref, slot, half):
    rows = ref.shape[1]
    if half is None:
        return ref.at[slot]
    return ref.at[slot, pl.ds(half * (rows // 2), rows // 2)]


def pair_view(ref, slot, half):
    if half is None:
        return ref.at[:, slot]
    return ref.at[half, slot]


def plane_view(ref, slot, part, half):
    rows, cols = ref.shape[-2] // 2, ref.shape[-1] // 2
    where = () if slot is None else (slot,)
    if half is None:
        return ref.at[(*where, slice(None), pl.ds(part * cols, cols))]
    return ref.at[(*where, pl.ds(half * rows, rows), pl.ds(part * cols, cols))]


def gather_kernel(views, planes, *refs):
    packs = len(views)
    total = packs + planes
    ins, outs = refs[:total], refs[total : 2 * total]
    net = Net(*refs[2 * total :])
    net.greet((["core", "y"] if packs else []) + (["x", "z"] if planes else []))
    steps, start = [], 0.0
    for i in range(planes):
        inp, out = ins[packs + i], outs[packs + i]
        u = us(inp.shape[0] * inp.shape[1] // 2)
        for part in range(2):
            steps.append(gather_plane(net, inp, out, plane_view, part, start, u))
        start += u / 2
    sizes = [us(functools.reduce(lambda a, b: a * b, r.shape)) for r in ins[:packs]]
    start = 0.0
    for i in range(packs):
        steps.append(gather_pack(net, ins[i], outs[i], views[i], start, sizes[i], sum(sizes)))
        start += sizes[i]
    in_turn(steps)
    net.finish()


def gather(ident, pack_arrays, plane_arrays):
    views, outs = [], []
    for a in pack_arrays:
        if a.ndim == 2:
            views.append(rows_view)
            outs.append(jax.ShapeDtypeStruct((8, *a.shape), a.dtype))
        else:
            views.append(pair_view)
            outs.append(jax.ShapeDtypeStruct((a.shape[0], 8, *a.shape[1:]), a.dtype))
    for a in plane_arrays:
        outs.append(jax.ShapeDtypeStruct((16, *a.shape), a.dtype))
    n, m = len(pack_arrays), len(plane_arrays)
    result = call(
        functools.partial(gather_kernel, tuple(views), m),
        ident,
        [*pack_arrays, *plane_arrays],
        outs,
        [ANY] * (n + m),
        [ANY] * (n + m),
        [],
        9 * n + 40 * m,
        n + 2 * m,
    )
    packed = []
    for a, r in zip(pack_arrays, result[:n]):
        if a.ndim == 2:
            packed.append(r.reshape(8 * a.shape[0], a.shape[1]))
        else:
            packed.append(r.reshape(a.shape[0], 8 * a.shape[1], a.shape[2]))
    return packed, result[n:]


def put_into(ref):
    def put(half, value):
        ref[half] = value.astype(ref.dtype)

    return put


def block_view(ref, slot):
    return ref.at[slot]


def pair_block_view(ref, slot):
    return ref.at[:, slot]


def scatter_kernel(kinds, planes, swaps, finals, ready, blocked, *refs):
    refs = list(refs)
    take = lambda n: [refs.pop(0) for _ in range(n)]
    packs = len(kinds)
    pack_in, plane_in, swap_in, ready_in = take(packs), take(planes), take(swaps), take(ready)
    pack_out, plane_out, swap_out, ready_out = take(packs), take(planes), take(swaps), take(ready)
    pack_scratch = [take(3) for _ in range(packs)]
    plane_scratch = [[take(3) for _ in range(2)] for _ in range(planes)]
    small = [finals and r.shape[-1] == 128 for r in pack_in]
    final_scratch = [take(2) for _ in range(packs)] if finals else []
    ready_scratch = [take(1) for _ in range(ready)]
    net = Net(*refs)
    wide = planes or swaps or finals
    net.greet(
        (["core", "y"] if packs else []) + (["x", "z"] if wide else []),
        group=bool(swaps or finals),
    )
    steps = []
    for i in range(planes):
        for part in range(2):
            cols = plane_in[i].shape[2] // 2

            def put(half, value, i=i, part=part, cols=cols):
                rows = plane_in[i].shape[1] // 2
                plane_out[i][
                    half * rows : (half + 1) * rows, part * cols : (part + 1) * cols
                ] = value.astype(plane_out[i].dtype)

            steps.append(sum_plane(net, part, plane_in[i], cols, put, *plane_scratch[i][part]))
    for i in range(swaps):
        steps.append(swap_small(net, swap_in[i], swap_out[i]))

    def put_blocks(ref):
        def put(half, value):
            n = value.shape[-1] // 2
            for r in range(4):
                for c in range(2):
                    ref[(half * 4 + r) * 2 + c] = value[
                        r * 16 : (r + 1) * 16, c * n : (c + 1) * n
                    ].astype(BF)

        return put

    def put_narrow(ref):
        def put(half, value):
            ref[half * 8 : half * 8 + 8] = value.reshape(8, 8, 128)

        return put

    def dense(i, start, b):
        whole, landed = final_scratch[i]
        put = put_narrow(whole) if small[i] else put_blocks(whole)
        yield from sum_pack(net, pack_in[i], kinds[i], put, start, b, *pack_scratch[i])
        yield from sum_all(net, whole, pack_out[i], start + 1.5 * b + 4, landed)

    for i in range(ready):
        steps.append(sum_all(net, ready_in[i], ready_out[i], 3.0, *ready_scratch[i]))
    start = 0.0
    for i in range(packs):
        values = functools.reduce(lambda a, b: a * b, pack_in[i].shape) // 8
        b = us(values)
        scratch = pack_scratch[i]
        if not finals:
            put = put_blocks(pack_out[i]) if i in blocked else put_into(pack_out[i])
            steps.append(sum_pack(net, pack_in[i], kinds[i], put, start, b, *scratch))
        else:
            steps.append(dense(i, start, b))
        start += 1.5 * b
    in_turn(steps)
    net.finish()


def scatter(
    ident, pack_arrays, plane_arrays, swap_arrays=(), finals=False, ready=(), blocked=()
):
    kinds, outs, scratch, keeps = [], [], [], len(swap_arrays)
    for a in pack_arrays:
        if a.shape[0] == 2:
            kinds.append(pair_block_view)
            block = (2, *a.shape[2:])
        else:
            kinds.append(block_view)
            block = a.shape[1:]
        half = block[1:]
        if finals and block[-1] == 128:
            outs.append(jax.ShapeDtypeStruct((16, 8, 128), F32))
        elif finals or len(outs) in blocked:
            outs.append(jax.ShapeDtypeStruct((16, 16, block[-1] // 2), BF))
        else:
            outs.append(jax.ShapeDtypeStruct(block, BF))
        scratch += [
            pltpu.VMEM((4, *block), BF),
            pltpu.VMEM((6, *half), BF),
            pltpu.VMEM((2, *half), BF),
        ]
    for a in plane_arrays:
        rows, cols = a.shape[1] // 2, a.shape[2] // 2
        outs.append(jax.ShapeDtypeStruct(a.shape[1:], F32))
        for _ in range(2):
            scratch += [
                pltpu.VMEM((5, 6, rows, cols), BF),
                pltpu.VMEM((5, 2, rows, cols), BF),
                pltpu.VMEM((4, 2, rows, cols), BF),
            ]
    for a in swap_arrays:
        outs.append(jax.ShapeDtypeStruct(a.shape, a.dtype))
    events = 10 * len(pack_arrays) + 60 * len(plane_arrays) + 15 * len(swap_arrays)
    if finals:
        for a in pack_arrays:
            n = a.shape[-1]
            whole = pltpu.VMEM((16, 8, 128), F32) if n == 128 else pltpu.VMEM((16, 16, n // 2), BF)
            scratch += [whole, whole]
            events += 30
    for a in ready:
        outs.append(jax.ShapeDtypeStruct(a.shape, BF))
        scratch.append(pltpu.VMEM(a.shape, BF))
        events += 30
    ins = [*pack_arrays, *plane_arrays, *swap_arrays, *ready]
    return call(
        functools.partial(
            scatter_kernel,
            tuple(kinds),
            len(plane_arrays),
            len(swap_arrays),
            finals,
            len(ready),
            blocked,
        ),
        ident,
        ins,
        outs,
        [INSIDE] * len(ins),
        [INSIDE] * len(ins),
        scratch,
        events,
        keeps,
    )


KEYS = 8 * ROWS
BLOCK = 256
FOUR = 4 * ROWS


def dot_last(a, b):
    return lax.dot_general(a, b, (((1,), (1,)), ((), ())), preferred_element_type=F32)


def dot_first(a, b):
    return lax.dot_general(a, b, (((0,), (0,)), ((), ())), preferred_element_type=F32)


def low_lanes(rows):
    return lax.broadcasted_iota(jnp.int32, (rows, 128), 1) < HEAD_SIZE


def four_heads(v):
    low = low_lanes(ROWS)
    a, b = v[:, :128], v[:, 128:]
    zero = jnp.zeros_like(a)
    return jnp.concatenate(
        [
            jnp.where(low, a, zero),
            jnp.where(low, pltpu.roll(a, HEAD_SIZE, 1), zero),
            jnp.where(low, zero, pltpu.roll(b, HEAD_SIZE, 1)),
            jnp.where(low, zero, b),
        ],
        axis=0,
    )


def side_by_side(v):
    low = low_lanes(ROWS)
    r = [v[i * ROWS : (i + 1) * ROWS] for i in range(4)]
    return jnp.concatenate(
        [
            jnp.where(low, r[0], pltpu.roll(r[1], HEAD_SIZE, 1)),
            jnp.where(low, pltpu.roll(r[2], HEAD_SIZE, 1), r[3]),
        ],
        axis=1,
    )


def set_bias(span_ref, bias):
    @pl.when(pl.program_id(0) == 0)
    def _():
        first, last = span_ref[0:1, :], span_ref[1:2, :]
        for b in range(0, KEYS, BLOCK):
            at = lax.broadcasted_iota(jnp.int32, (BLOCK, FOUR), 0) + b
            bias[b : b + BLOCK] = jnp.where((at >= first) & (at <= last), 0.0, -1e30)


def attend_kernel(q_ref, k_ref, v_ref, span_ref, o_ref, lse_ref, bias, score):
    set_bias(span_ref, bias)
    q = four_heads(q_ref[...].astype(F32) * HEAD_SIZE ** (-0.5)).astype(BF)
    top = jnp.full((1, FOUR), -3e38, F32)
    for b in range(0, KEYS, BLOCK):
        s = dot_last(k_ref[b : b + BLOCK], q) + bias[b : b + BLOCK]
        score[b : b + BLOCK] = s
        top = jnp.maximum(top, jnp.max(s, axis=0, keepdims=True))
    total = jnp.zeros((1, FOUR), F32)
    out = jnp.zeros((128, FOUR), F32)
    for b in range(0, KEYS, BLOCK):
        e = jnp.exp(score[b : b + BLOCK] - top)
        total = total + jnp.sum(e, axis=0, keepdims=True)
        out = out + dot_first(v_ref[b : b + BLOCK], e.astype(BF))
    o_ref[...] = side_by_side((out / total).T).astype(BF)
    lse_ref[0] = jnp.broadcast_to(top + jnp.log(total), (8, FOUR))


def attend(query, kv, span):
    return pl.pallas_call(
        attend_kernel,
        grid=(4,),
        in_specs=[
            pl.BlockSpec((ROWS, 256), lambda p: (0, p)),
            pl.BlockSpec((KEYS, 128), lambda p: (0, p)),
            pl.BlockSpec((KEYS, 128), lambda p: (0, 4 + p)),
            pl.BlockSpec((8, FOUR), lambda p: (0, 0)),
        ],
        out_specs=[
            pl.BlockSpec((ROWS, 256), lambda p: (0, p)),
            pl.BlockSpec((1, 8, FOUR), lambda p: (p, 0, 0)),
        ],
        out_shape=[
            jax.ShapeDtypeStruct((ROWS, WIDTH), BF),
            jax.ShapeDtypeStruct((4, 8, FOUR), F32),
        ],
        scratch_shapes=[pltpu.VMEM((KEYS, FOUR), F32), pltpu.VMEM((KEYS, FOUR), F32)],
        compiler_params=pltpu.CompilerParams(vmem_limit_bytes=48 << 20),
    )(query, kv, kv, span)


def attend_back_kernel(
    q_ref, k_ref, v_ref, g_ref, o_ref, lse_ref, span_ref, dq_ref, dk_ref, dv_ref, bias
):
    set_bias(span_ref, bias)
    q = four_heads(q_ref[...].astype(F32) * HEAD_SIZE ** (-0.5)).astype(BF)
    wide = four_heads(g_ref[...].astype(F32))
    g = wide.astype(BF)
    spread = jnp.sum((wide * four_heads(o_ref[...].astype(F32))).T, axis=0, keepdims=True)
    lse = lse_ref[0, 0:1, :]
    dq = jnp.zeros((128, FOUR), F32)
    for b in range(0, KEYS, BLOCK):
        k = k_ref[b : b + BLOCK]
        p = jnp.exp(dot_last(k, q) + bias[b : b + BLOCK] - lse)
        dp = dot_last(v_ref[b : b + BLOCK], g)
        ds = (p * (dp - spread)).astype(BF)
        dv_ref[b : b + BLOCK] = jnp.dot(p.astype(BF), g, preferred_element_type=F32).astype(BF)
        dk_ref[b : b + BLOCK] = jnp.dot(ds, q, preferred_element_type=F32).astype(BF)
        dq = dq + dot_first(k, ds)
    dq_ref[...] = side_by_side(dq.T * HEAD_SIZE ** (-0.5))


def attend_back(query, kv, grad, attended, lse, span):
    return pl.pallas_call(
        attend_back_kernel,
        grid=(4,),
        in_specs=[
            pl.BlockSpec((ROWS, 256), lambda p: (0, p)),
            pl.BlockSpec((KEYS, 128), lambda p: (0, p)),
            pl.BlockSpec((KEYS, 128), lambda p: (0, 4 + p)),
            pl.BlockSpec((ROWS, 256), lambda p: (0, p)),
            pl.BlockSpec((ROWS, 256), lambda p: (0, p)),
            pl.BlockSpec((1, 8, FOUR), lambda p: (p, 0, 0)),
            pl.BlockSpec((8, FOUR), lambda p: (0, 0)),
        ],
        out_specs=[
            pl.BlockSpec((ROWS, 256), lambda p: (0, p)),
            pl.BlockSpec((KEYS, 128), lambda p: (0, p)),
            pl.BlockSpec((KEYS, 128), lambda p: (0, p)),
        ],
        out_shape=[
            jax.ShapeDtypeStruct((ROWS, WIDTH), F32),
            jax.ShapeDtypeStruct((KEYS, 512), BF),
            jax.ShapeDtypeStruct((KEYS, 512), BF),
        ],
        scratch_shapes=[pltpu.VMEM((KEYS, FOUR), F32)],
        compiler_params=pltpu.CompilerParams(vmem_limit_bytes=48 << 20),
    )(query, kv, kv, grad, attended, lse, span)


AT_ONCE = 4
STEP_ROWS = AT_ONCE * SLOTS


def experts_kernel(
    routed_ref,
    up_ref,
    info_ref,
    gate_ref,
    lift_ref,
    down_ref,
    out0_ref,
    out1_ref,
    back_ref,
    dots_ref,
    grad_gate_ref,
    grad_lift_ref,
    grad_down_ref,
    sum_gate,
    sum_lift,
    sum_down,
):
    @pl.when(pl.program_id(0) == 0)
    def _():
        sum_gate[...] = jnp.zeros_like(sum_gate)
        sum_lift[...] = jnp.zeros_like(sum_lift)
        sum_down[...] = jnp.zeros_like(sum_down)

    place = lax.broadcasted_iota(jnp.int32, (SLOTS, ROWS), 0).astype(F32)
    picks, rows, ups, gates = [], [], [], []
    for s in range(AT_ONCE):
        info = info_ref[s]
        halves = [(place == info[j : j + 1, :]).astype(F32) for j in range(2)]
        gates.append(
            [jnp.sum(halves[j] * info[2 + j : 3 + j, :], axis=1, keepdims=True) for j in range(2)]
        )
        pick = jnp.concatenate(halves, axis=0).astype(BF)
        picks.append((pick, halves))
        rows.append(jnp.dot(pick, routed_ref[s], preferred_element_type=F32).astype(BF))
        ups.append(jnp.dot(pick, up_ref[s], preferred_element_type=F32).astype(BF))

    def of(j, parts):
        return jnp.concatenate([p[j * SLOTS : (j + 1) * SLOTS] for p in parts], axis=0)

    weighed, back, dots = [], [], []
    for j in range(2):
        x, up = of(j, rows), of(j, ups).astype(F32)
        share = jnp.concatenate([g[j] for g in gates], axis=0)
        a = jnp.dot(x, gate_ref[j], preferred_element_type=F32)
        b = jnp.dot(x, lift_ref[j], preferred_element_type=F32)
        sig = 1.0 / (1.0 + jnp.exp(-a))
        silu = a * sig
        inner = (silu * b).astype(BF)
        produced = jnp.dot(inner, down_ref[j], preferred_element_type=F32)
        produced = produced.astype(BF).astype(F32)
        dots.append(jnp.sum(produced * up, axis=1, keepdims=True))
        weighed.append((share * produced).astype(BF))
        grad = (share * up).astype(BF)
        grad_inner = dot_last(grad, down_ref[j])
        grad_a = (grad_inner * b * sig * (1.0 + a * (1.0 - sig))).astype(BF)
        grad_b = (grad_inner * silu).astype(BF)
        back.append((dot_last(grad_a, gate_ref[j]) + dot_last(grad_b, lift_ref[j])).astype(BF))
        sum_gate[j] += dot_first(x, grad_a)
        sum_lift[j] += dot_first(x, grad_b)
        sum_down[j] += dot_first(inner, grad)
    for s in range(AT_ONCE):
        pick, halves = picks[s]
        span = slice(s * SLOTS, (s + 1) * SLOTS)
        both = jnp.concatenate([weighed[0][span], weighed[1][span]], axis=0)
        out = dot_first(pick, both)
        out0_ref[s] = out[:, : WIDTH // 2].astype(BF)
        out1_ref[s] = out[:, WIDTH // 2 :].astype(BF)
        both = jnp.concatenate([back[0][span], back[1][span]], axis=0)
        back_ref[s] = dot_first(pick, both).astype(BF)
        for j in range(2):
            line = jnp.sum(halves[j] * dots[j][span], axis=0, keepdims=True)
            dots_ref[s, j : j + 1, :ROWS] = line

    @pl.when(pl.program_id(0) == 16 // AT_ONCE - 1)
    def _():
        grad_gate_ref[...] = sum_gate[...].astype(BF)
        grad_lift_ref[...] = sum_lift[...].astype(BF)
        grad_down_ref[...] = sum_down[...].astype(BF)


def run_experts(routed, up, info, gate, lift, down):
    wide = pl.BlockSpec((AT_ONCE, ROWS, WIDTH), lambda i: (i, 0, 0))
    half = pl.BlockSpec((AT_ONCE, ROWS, WIDTH // 2), lambda i: (i, 0, 0))
    once = lambda shape: pl.BlockSpec(shape, lambda i: (0, 0, 0))
    kept = lambda shape: pl.BlockSpec(
        shape, lambda i: (0, 0, 0), pipeline_mode=pl.Buffered(buffer_count=1)
    )
    tall, flat = (2, WIDTH, 512), (2, 512, WIDTH)
    return pl.pallas_call(
        experts_kernel,
        grid=(16 // AT_ONCE,),
        in_specs=[
            wide,
            wide,
            pl.BlockSpec((AT_ONCE, 8, ROWS), lambda i: (i, 0, 0)),
            kept(tall),
            kept(tall),
            kept(flat),
        ],
        out_specs=[
            half,
            half,
            wide,
            pl.BlockSpec((AT_ONCE, 8, LANES), lambda i: (i, 0, 0)),
            once(tall),
            once(tall),
            once(flat),
        ],
        out_shape=[
            jax.ShapeDtypeStruct((16, ROWS, WIDTH // 2), BF),
            jax.ShapeDtypeStruct((16, ROWS, WIDTH // 2), BF),
            jax.ShapeDtypeStruct((16, ROWS, WIDTH), BF),
            jax.ShapeDtypeStruct((16, 8, LANES), F32),
            jax.ShapeDtypeStruct(tall, BF),
            jax.ShapeDtypeStruct(tall, BF),
            jax.ShapeDtypeStruct(flat, BF),
        ],
        scratch_shapes=[pltpu.VMEM(tall, F32), pltpu.VMEM(tall, F32), pltpu.VMEM(flat, F32)],
        compiler_params=pltpu.CompilerParams(vmem_limit_bytes=60 << 20),
    )(routed, up, info, gate, lift, down)


def contract_first(left_op, right_op):
    return lax.dot_general(left_op, right_op, (((0,), (0,)), ((), ())), preferred_element_type=F32)


def contract_last(left_op, right_op):
    return lax.dot_general(left_op, right_op, (((1,), (1,)), ((), ())), preferred_element_type=F32)


def rotary(offset, width):
    half_dim = HEAD_SIZE // 2
    lane = jnp.arange(width, dtype=jnp.int32)
    frequency = BASE ** (-2.0 * (lane % half_dim).astype(F32) / HEAD_SIZE)
    angles = offset.astype(F32)[:, None] * frequency[None, :]
    return jnp.cos(angles), jnp.sin(angles)


def swapped(v):
    half_dim = HEAD_SIZE // 2
    first = (jnp.arange(v.shape[1], dtype=jnp.int32) % HEAD_SIZE < half_dim)[None, :]
    return jnp.where(first, -jnp.roll(v, -half_dim, axis=1), jnp.roll(v, half_dim, axis=1))


def norm_back(inputs, inverse_rms, gain_vec, upstream):
    scaled = upstream * gain_vec
    gain_grad = jnp.sum(upstream * inputs * inverse_rms, axis=0)
    spread = jnp.mean(scaled * inputs, axis=-1, keepdims=True)
    return (inverse_rms * scaled - inputs * inverse_rms**3 * spread, gain_grad)


def mm(pattern, a, b):
    return jnp.einsum(pattern, a, b, preferred_element_type=F32)


def shards(
    hidden_in,
    grad_out,
    lengths,
    experts,
    gain_attn,
    w_query,
    key_weight,
    value_weight,
    w_out,
    gain_moe,
    w_router,
    expert_gate,
    expert_up,
    expert_down,
):
    fsdp = lax.axis_index("fsdp")
    owner = lax.axis_index("expert")
    inputs = hidden_in[0].astype(F32)
    upstream = grad_out[0].astype(F32)
    picked = experts[0]

    named = jnp.any(
        picked[None, :, :] == jnp.arange(EXPERTS, dtype=jnp.int32)[:, None, None], axis=-1
    )
    named_wide = jnp.pad(named.astype(BF), ((0, 0), (0, LANES - ROWS)))
    small = jnp.concatenate(
        [w_router, gain_attn[:, None], gain_moe[:, None], jnp.zeros((128, 94), BF)], axis=1
    )
    (full_query, full_key, full_value, full_out, full_small), (all_up, all_named) = gather(
        0, [w_query, key_weight, value_weight, w_out, small], [grad_out[0], named_wide]
    )
    full_router = full_small[:, :EXPERTS]
    full_gain_a = full_small[:, EXPERTS].astype(F32)
    full_gain_m = full_small[:, EXPERTS + 1].astype(F32)

    seq_lengths = lengths[0]
    seq_ends = jnp.cumsum(seq_lengths, dtype=jnp.int32)
    starts = seq_ends - seq_lengths

    def places(index):
        inside = (index[:, None] >= starts[None, :]) & (index[:, None] < seq_ends[None, :])
        inside = inside.astype(jnp.int32)
        return jnp.sum(inside * (index[:, None] - starts[None, :]), axis=1)

    own_index = fsdp * ROWS + jnp.arange(ROWS, dtype=jnp.int32)
    own_offset = places(own_index)
    cosine, sine = lax.optimization_barrier(rotary(own_offset, 128))
    cosine, sine = jnp.tile(cosine, (1, 8)), jnp.tile(sine, (1, 8))
    cosine_k, sine_k = cosine[:, :512], sine[:, :512]
    span = jnp.concatenate(
        [
            jnp.tile(own_index - own_offset, 4)[None, :],
            jnp.tile(own_index, 4)[None, :],
            jnp.zeros((6, FOUR), jnp.int32),
        ]
    )

    inverse_a = lax.rsqrt(jnp.mean(inputs * inputs, axis=-1, keepdims=True) + EPS)
    normed = (inputs * inverse_a * full_gain_a).astype(BF)
    query = jnp.dot(normed, full_query, preferred_element_type=F32)
    key = jnp.dot(normed, full_key, preferred_element_type=F32)
    value = jnp.dot(normed, full_value, preferred_element_type=F32).astype(BF)
    query = (query * cosine + swapped(query) * sine).astype(BF)
    key = (key * cosine_k + swapped(key) * sine_k).astype(BF)
    (kv,), _ = gather(1, [jnp.concatenate([key, value], axis=1)], [])
    attended, lse = attend(query, kv, span)
    hidden = inputs + jnp.dot(attended, full_out, preferred_element_type=F32)
    inverse_m = lax.rsqrt(jnp.mean(hidden * hidden, axis=-1, keepdims=True) + EPS)
    routed = (hidden * inverse_m * full_gain_m).astype(BF)

    (full_gate, full_up, full_down), (all_routed,) = gather(
        2, [expert_gate, expert_up, expert_down], [routed]
    )
    all_named = all_named[:, :, :ROWS]
    logits = mm("de,std->set", full_router, all_routed)
    logits = jnp.where(all_named > 0, logits, -1e30)
    own_logits = lax.dynamic_slice_in_dim(logits, 2 * owner, 2, axis=1)
    own_named = lax.dynamic_slice_in_dim(all_named, 2 * owner, 2, axis=1)
    top = jnp.max(logits, axis=1, keepdims=True)
    total = jnp.sum(jnp.exp(logits - top), axis=1, keepdims=True)
    own_gates = jnp.exp(own_logits - top) / total * own_named.astype(F32)
    before = (
        jnp.arange(ROWS, dtype=jnp.int32)[:, None] < jnp.arange(ROWS, dtype=jnp.int32)[None, :]
    ).astype(BF)
    rank = jnp.where(own_named > 0, mm("sjt,tu->sju", own_named, before), -1.0)
    info = jnp.concatenate([rank, own_gates, jnp.zeros((16, 4, ROWS), F32)], axis=1)
    out_low, out_high, part_grad, token_dots, grad_gate_w, grad_up_w, grad_down_w = run_experts(
        all_routed, all_up, info, full_gate, full_up, full_down
    )
    sum_gate, sum_up, sum_down, grad_routed, dots = scatter(
        3,
        [
            grad_gate_w.reshape(2, 8, 128, 512),
            grad_up_w.reshape(2, 8, 128, 512),
            grad_down_w.reshape(2, 8, 64, 1024),
        ],
        [part_grad],
        [token_dots],
    )

    dots = dots[:, :2, :ROWS].reshape(EXPERTS, ROWS)
    here = jnp.where(named, contract_last(full_router.T, routed), -1e30)
    here = jnp.exp(here - jnp.max(here, axis=0, keepdims=True)) * named.astype(F32)
    gates = here / jnp.sum(here, axis=0, keepdims=True)
    grad_logits = (gates * (dots - jnp.sum(gates * dots, axis=0, keepdims=True))).astype(BF)
    grad_routed = grad_routed + mm("et,de->td", grad_logits, full_router)
    grad_router_w = mm("td,et->de", routed, grad_logits)
    grad_middle, grad_gain_m = norm_back(hidden, inverse_m, full_gain_m, grad_routed)
    grad_hidden = upstream + grad_middle
    grad_hidden_low = grad_hidden.astype(BF)
    grad_out_w = contract_first(attended, grad_hidden_low)
    grad_attended = contract_last(grad_hidden_low, full_out).astype(BF)
    grad_query, grad_key, grad_value = attend_back(query, kv, grad_attended, attended, lse, span)
    block = lambda a: a.reshape(8, 2, 64, a.shape[-1])
    grad_key, grad_value, sum_out, moe_low = scatter(
        4,
        [
            grad_key.reshape(8, 2, 80, 512),
            grad_value.reshape(8, 2, 80, 512),
            block(grad_out_w.astype(BF)),
        ],
        [out_low],
        blocked=(2,),
    )
    grad_key = grad_key.reshape(ROWS, 512).astype(F32)
    grad_value = grad_value.reshape(ROWS, 512)
    grad_query = (grad_query * cosine - swapped(grad_query) * sine).astype(BF)
    grad_key = (grad_key * cosine_k - swapped(grad_key) * sine_k).astype(BF)
    grad_kv = jnp.concatenate([grad_key, grad_value], axis=1)
    grad_query_w = contract_first(normed, grad_query).astype(BF)
    grad_kv_w = contract_first(normed, grad_kv).astype(BF)
    grad_normed = (
        contract_last(grad_query, full_query)
        + contract_last(grad_key, full_key)
        + contract_last(grad_value, full_value)
    )
    grad_first, grad_gain_a = norm_back(inputs, inverse_a, full_gain_a, grad_normed)
    grad_input = (grad_hidden + grad_first).astype(BF)
    grad_small = jnp.concatenate(
        [
            grad_router_w.astype(BF),
            grad_gain_a.astype(BF)[:, None],
            grad_gain_m.astype(BF)[:, None],
            jnp.zeros((WIDTH, 128 - 34), BF),
        ],
        axis=1,
    )
    tot_query, tot_kv, tot_small, moe_high, tot_out = scatter(
        5,
        [block(grad_query_w), block(grad_kv_w), block(grad_small)],
        [out_high],
        finals=True,
        ready=[sum_out],
    )
    output = (hidden + jnp.concatenate([moe_low, moe_high], axis=1)).astype(BF)
    flat = lambda a: a.reshape(8, 2, 16, 512).transpose(0, 2, 1, 3).reshape(128, 1024).astype(F32)
    parts = tot_kv.reshape(8, 2, 16, 512)
    tot_key, tot_value = [parts[:, i].reshape(128, 512).astype(F32) for i in range(2)]
    tot_small = tot_small.reshape(128, 128)
    return (
        output[None],
        grad_input[None],
        tot_small[:, EXPERTS],
        flat(tot_query),
        tot_key,
        tot_value,
        flat(tot_out),
        tot_small[:, EXPERTS + 1],
        tot_small[:, :EXPERTS],
        sum_gate.astype(F32),
        sum_up.astype(F32),
        sum_down.astype(F32),
    )


def solution(mesh):
    token, matrix, stack = P("expert", "fsdp", None), P("fsdp", None), P("expert", "fsdp", None)
    return jax.shard_map(
        shards,
        mesh=mesh,
        in_specs=(
            token,
            token,
            P("expert", None),
            token,
            P("fsdp"),
            matrix,
            matrix,
            matrix,
            matrix,
            P("fsdp"),
            matrix,
            stack,
            stack,
            stack,
        ),
        out_specs=(
            token,
            token,
            P("fsdp"),
            matrix,
            matrix,
            matrix,
            matrix,
            P("fsdp"),
            matrix,
            stack,
            stack,
            stack,
        ),
        check_vma=False,
    )
```
